32 devices in a mesh: dp: 2 (over y), expert: 16 (over z, x, core).
Axes of the slice: x: 2, y: 2, z: 4, core: 2. Of those that a mesh axis runs over, the one named last changes fastest.
Arguments:
- out_grad: bfloat16 [512, 4096], P(('dp', 'expert')), may hold values from -6 to 6
- hidden_acts: bfloat16 [512, 8, 768], P(('dp', 'expert')), may hold values from -0.23925781 to 0.23925781
- gate_weights: float32 [512, 8], P(('dp', 'expert')), may hold values from 0 to 1, as said below
- expert_idx: int32 [512, 8], P(('dp', 'expert')), may hold values from 0 to 15, all different within a row; in each aligned block of 16 rows (0 to 15, 16 to 31, ...) at most 12 rows name the same one
- down_weight: bfloat16 [16, 768, 4096], P('expert'), may hold values from -0.09375 to 0.09375
Outputs:
- act_grad: bfloat16 [512, 8, 768], P(('dp', 'expert'))
- logit_grad: float32 [512, 8], P(('dp', 'expert'))
- down_grad: bfloat16 [16, 768, 4096], P('expert', 'dp')
The draws below stay inside these ranges and needn't reach their ends.
Inputs may be any that keep to these rules, and one draw needn't show every extreme that they name: `expert_idx`: each row names 8 different experts; among the 16 rows of one device no expert is named more than 12 times, a bound that some block reaches. `gate_weights`: each row is positive and sums to one.
All inputs are finite; a program needn't handle non-finite values.
Results may differ from the reference program's by a relative error of at most 0.022.
Values may be sent and summed in bfloat16 or wider, within the bound.
A program may use at most 64 MiB of HBM per device.

```python
import math
import jax
import jax.numpy as jnp
import numpy as np
from jax import lax

D = 4096
TOP = 8
FW = 768
TOK_DEV = 16
EXPERTS = 16
MOST = 12
GROUP_TOK = 256
TOKENS = 512
N_DP = 2
N_EXPERT = 16


def draw_gate_weights(key, part):
    key = jax.random.fold_in(key, 5)
    logits = jnp.clip(0.4 * jax.random.normal(key, (TOKENS, TOP), jnp.float32), -0.8, 0.8)
    powers = jnp.exp(logits)
    return powers / jnp.sum(powers, axis=1, keepdims=True)


def block_scale(own_key, dims, cuts, least, high):
    level = 1.0
    for axis_at, shards_of in cuts:
        steps = jax.random.uniform(jax.random.fold_in(jax.random.fold_in(own_key, 6), axis_at), (shards_of,), jnp.float32, least / len(cuts), high / len(cuts))
        level = level * jnp.repeat(jnp.exp(steps), dims[axis_at] // shards_of).reshape((-1,) + (1,) * (len(dims) - 1 - axis_at))
    return level


def deal_out(own_key, own, number, rows, count, top, limit, skew):
    sequence = jax.random.permutation(own_key, count)
    packed, ordinary = load_shares(count, rows * top, limit, skew, True), load_shares(count, rows * top, limit, skew, False)
    places = jnp.arange(count)

    def named(tallies, rotation):
        used = int((tallies > 0).sum())
        fixed = max(1, used // 4)
        shifted = fixed + (places - fixed + rotation * (used - fixed)) % max(1, count - fixed)
        return jnp.zeros((count,), jnp.int32).at[sequence[jnp.where(places < fixed, places, shifted)]].set(jnp.asarray(tallies, jnp.int32))

    tallies = jnp.where(number % 4 == 0, named(packed, number // 4), named(ordinary, number - number // 4 - 1))
    mixed = jax.random.permutation(jax.random.fold_in(own, 3), count)
    donor, receiver = mixed[0:count // 2 * 2:2], mixed[1:count // 2 * 2:2]
    slack = jnp.minimum(tallies[donor] - 1, limit - tallies[receiver]) // 2
    slack = jnp.where((donor == sequence[0]) | (receiver == sequence[0]) | (tallies[receiver] == 0), 0, jnp.maximum(slack, 0))
    shifted = jax.random.randint(jax.random.fold_in(own, 4), (count // 2,), 0, 1 << 20) % (slack + 1)
    tallies = tallies.at[donor].add(-shifted).at[receiver].add(shifted)
    items = jnp.searchsorted(jnp.cumsum(tallies), jnp.arange(rows * top), side="right").astype(jnp.int32)
    grid = items.reshape(top, rows).T
    grid = grid[jax.random.permutation(jax.random.fold_in(own, 1), rows)]
    rotation = jax.random.randint(jax.random.fold_in(own, 2), (rows, 1), 0, top)
    return jnp.take_along_axis(grid, (jnp.arange(top)[None, :] + rotation) % top, axis=1)


def load_shares(number_of, total, bound, lean, full):
    portions = [(1 << 20) // math.isqrt(standing ** lean) + 1 for standing in range(1, number_of + 1)]
    largest = bound if full else min(bound, max(-(-total // number_of), total * portions[0] // sum(portions)))
    least = 1 if total - largest >= number_of - 1 else 0
    given, spare = [largest] + [least] * (number_of - 1), total - largest - least * (number_of - 1)
    while spare > 0:
        free = [i for i in range(1, number_of) if given[i] < largest] or [i for i in range(1, number_of) if given[i] < bound]
        whole, left = sum([portions[i] for i in free]), spare
        for i in free:
            extra = min(bound - given[i], max(1, left * portions[i] // whole), spare)
            given[i] = given[i] + extra
            spare = spare - extra
    return np.array(given)


def bell_draw(key, shape, deviation, most, shards=(), kind=jnp.bfloat16):
    entries = jax.random.normal(key, shape, jnp.float32) * deviation
    if len(shards) > 0:
        entries = block_scale(key, shape, shards, -0.22, 0.18) * entries
    return jnp.clip(entries, min=-most, max=most).astype(kind)


def setup_inputs(seed: int = 0) -> dict:
    keys = jax.random.split(jax.random.key(seed), 6)
    out_grad = bell_draw(keys[0], (TOKENS, D), 1.0, 6.0, ((0, 32),))
    hidden_acts = bell_draw(keys[1], (TOKENS, TOP, FW), 0.04, 0.23925781, ((0, 32),))
    gate_weights = draw_gate_weights(jax.random.fold_in(keys[5], 71), 0)
    expert_idx_keys = jax.random.split(jax.random.fold_in(keys[3], 1), TOKENS // TOK_DEV)
    expert_idx_turns = jax.random.permutation(jax.random.fold_in(keys[3], 3), TOKENS // TOK_DEV)
    expert_idx = jax.vmap(lambda own, number: deal_out(jax.random.fold_in(keys[3], 2), own, number, TOK_DEV, EXPERTS, TOP, MOST, 2))(expert_idx_keys, expert_idx_turns).reshape((TOKENS, TOP))
    down_weight = bell_draw(keys[4], (EXPERTS, FW, D), D ** -0.5, 0.09375, ((0, 16),))
    return dict(out_grad=out_grad, hidden_acts=hidden_acts, gate_weights=gate_weights, expert_idx=expert_idx, down_weight=down_weight)


def reference(out_grad, hidden_acts, gate_weights, expert_idx, down_weight):
    routed = TOKENS * TOP
    flat_expert = expert_idx.reshape(routed).astype(jnp.int32)
    row_ids = jnp.arange(routed, dtype=jnp.int32)
    group_of = (row_ids // (TOP * GROUP_TOK)).astype(jnp.int32)
    sort_keys = (flat_expert * N_DP + group_of).astype(jnp.int32)
    sorted_rows = jnp.argsort(sort_keys, stable=True).astype(jnp.int32)
    group_sizes = jnp.bincount(sort_keys, length=EXPERTS * N_DP).astype(jnp.int32)
    group_starts = (jnp.cumsum(group_sizes) - group_sizes).astype(jnp.int32)
    group_window = MOST * N_EXPERT
    padded_rows = jnp.concatenate([sorted_rows, jnp.full((group_window,), routed, jnp.int32)])
    gate_half = lax.optimization_barrier(gate_weights.astype(jnp.bfloat16)).astype(jnp.float32)
    flat_gate = jnp.concatenate([gate_half.reshape(routed), jnp.zeros((1,), jnp.float32)])
    flat_acts = jnp.concatenate([hidden_acts.reshape(routed, FW), jnp.zeros((1, FW), jnp.bfloat16)])
    grad_pad = jnp.concatenate([out_grad, jnp.zeros((1, D), jnp.bfloat16)])

    def expert_block(expert_id):
        expert_weight = down_weight[expert_id]

        def group_step(summed, group_id):
            key_now = expert_id * N_DP + group_id
            picked = lax.dynamic_slice(padded_rows, (group_starts[key_now].astype(jnp.int32),), (group_window,))
            is_live = jnp.arange(group_window, dtype=jnp.int32) < group_sizes[key_now]
            picked = jnp.where(is_live, picked, routed).astype(jnp.int32)
            token_ids = jnp.where(is_live, picked // TOP, TOKENS).astype(jnp.int32)
            grad_rows = grad_pad[token_ids]
            act_rows = flat_acts[picked]
            gate_rows = flat_gate[picked][:, None]
            grad_hidden = jnp.dot(grad_rows, expert_weight.T, preferred_element_type=jnp.float32)
            act_back = (gate_rows * grad_hidden).astype(jnp.bfloat16)
            score_back = jnp.sum(grad_hidden * act_rows.astype(jnp.float32), axis=1).astype(jnp.bfloat16)
            scaled_grad = (gate_rows * grad_rows.astype(jnp.float32)).astype(jnp.bfloat16)
            group_part = jnp.dot(act_rows.T, scaled_grad, preferred_element_type=jnp.float32).astype(jnp.bfloat16)
            return summed + group_part.astype(jnp.float32), (picked, act_back, score_back)

        summed, outputs = lax.scan(group_step, jnp.zeros((FW, D), jnp.float32), jnp.arange(N_DP, dtype=jnp.int32))
        return summed.astype(jnp.bfloat16), outputs[0], outputs[1], outputs[2]

    down_grad, picked, act_back, score_back = lax.map(expert_block, jnp.arange(EXPERTS, dtype=jnp.int32))
    target = picked.reshape(-1).astype(jnp.int32)
    act_grad = jnp.zeros((routed + 1, FW), jnp.bfloat16).at[target].set(act_back.reshape(-1, FW))[:routed]
    score = jnp.zeros((routed + 1,), jnp.float32).at[target].set(score_back.reshape(-1).astype(jnp.float32))[:routed]
    score = score.reshape(TOKENS, TOP)
    logit_grad = gate_weights * (score - jnp.sum(gate_weights * score, axis=1, keepdims=True))
    return act_grad.reshape(TOKENS, TOP, FW), logit_grad, down_grad
```

```python
import functools

import jax
import jax.numpy as jnp
from jax import lax
from jax.experimental import pallas as pl
from jax.experimental.pallas import tpu as pltpu
from jax.sharding import PartitionSpec as P

MESH = pl.DeviceIdType.MESH
ZS, XS, CS = 4, 2, 2


def routed_shards(out_grad, hidden_acts, gate_weights, expert_idx, down_weight):
    tok_rows, top_count = expert_idx.shape
    routed = tok_rows * top_count
    hidden_width = hidden_acts.shape[2]
    owners = lax.axis_size("expert")
    experts = owners * down_weight.shape[0]
    capacity = min(tok_rows, max(2, (3 * tok_rows * top_count + 2 * experts - 1) // (2 * experts)))
    slot_count = experts * capacity
    flat_expert = expert_idx.reshape(routed)
    member = (flat_expert[:, None] == jnp.arange(experts, dtype=jnp.int32)[None, :]).astype(
        jnp.bfloat16
    )
    row_line = jnp.arange(routed, dtype=jnp.int32)
    earlier_mask = (row_line[:, None] > row_line[None, :]).astype(jnp.bfloat16)
    earlier = jnp.dot(earlier_mask, member, preferred_element_type=jnp.float32)
    position = jnp.sum(earlier * member.astype(jnp.float32), axis=1).astype(jnp.int32)
    slot_index = flat_expert * capacity + position
    placement = (jnp.arange(slot_count, dtype=jnp.int32)[:, None] == slot_index[None, :]).astype(
        jnp.bfloat16
    )
    token_place = jnp.sum(placement.reshape(slot_count, tok_rows, top_count), axis=2)
    gate_half = lax.optimization_barrier(gate_weights.astype(jnp.bfloat16))
    send_grads = jnp.dot(token_place, out_grad, preferred_element_type=jnp.float32).astype(
        jnp.bfloat16
    )
    send_acts = jnp.dot(
        placement, hidden_acts.reshape(routed, hidden_width), preferred_element_type=jnp.float32
    ).astype(jnp.bfloat16)
    send_gate = jnp.dot(
        placement, gate_half.reshape(routed, 1), preferred_element_type=jnp.float32
    ).astype(jnp.bfloat16)
    grads_in, acts_in, gate_in = (
        lax.all_to_all(
            send_grads.reshape(owners, capacity, out_grad.shape[1]),
            "expert",
            split_axis=0,
            concat_axis=0,
            tiled=True,
        ),
        lax.all_to_all(
            send_acts.reshape(owners, capacity, hidden_width),
            "expert",
            split_axis=0,
            concat_axis=0,
            tiled=True,
        ),
        lax.all_to_all(
            send_gate.reshape(owners, capacity), "expert", split_axis=0, concat_axis=0, tiled=True
        ),
    )
    grads_in = grads_in.reshape(slot_count, out_grad.shape[1])
    acts_in = acts_in.reshape(slot_count, hidden_width)
    gate_rows = gate_in.reshape(slot_count, 1).astype(jnp.float32)
    expert_weight = down_weight[0]
    grad_hidden = lax.dot_general(
        grads_in, expert_weight, (((1,), (1,)), ((), ())), preferred_element_type=jnp.float32
    )
    act_back = (gate_rows * grad_hidden).astype(jnp.bfloat16)
    score_back = jnp.sum(grad_hidden * acts_in.astype(jnp.float32), axis=1).astype(jnp.bfloat16)
    scaled_grad = (gate_rows * grads_in.astype(jnp.float32)).astype(jnp.bfloat16)
    back_rows, back_scores = (
        lax.all_to_all(
            act_back.reshape(owners, capacity, hidden_width),
            "expert",
            split_axis=0,
            concat_axis=0,
            tiled=True,
        ),
        lax.all_to_all(
            score_back.reshape(owners, capacity), "expert", split_axis=0, concat_axis=0, tiled=True
        ),
    )
    weight_term = lax.dot_general(
        acts_in, scaled_grad, (((0,), (0,)), ((), ())), preferred_element_type=jnp.float32
    )
    summed = lax.psum_scatter(
        weight_term.astype(jnp.bfloat16), "dp", scatter_dimension=0, tiled=True
    )
    down_grad = summed[None]
    act_grad = lax.dot_general(
        placement,
        back_rows.reshape(slot_count, hidden_width),
        (((0,), (0,)), ((), ())),
        preferred_element_type=jnp.float32,
    ).astype(jnp.bfloat16)
    score_tok = lax.dot_general(
        placement,
        back_scores.reshape(slot_count, 1),
        (((0,), (0,)), ((), ())),
        preferred_element_type=jnp.float32,
    ).reshape(tok_rows, top_count)
    logit_grad = gate_weights * (
        score_tok - jnp.sum(gate_weights * score_tok, axis=1, keepdims=True)
    )
    return (act_grad.reshape(tok_rows, top_count, hidden_width), logit_grad, down_grad)


def slot_of(y, x, z, c):
    return y * (XS * ZS * CS) + x * (ZS * CS) + z * CS + c


def expert_of(x, z, c):
    return z * (XS * CS) + x * CS + c


def gather_kernel(
    gate_ref, idx_ref, acts_ref, grad_ref, w_hbm,
    act_out, logit_out, down_out,
    grads, w_buf, acts_send, acts_in, acts_t, hid, back,
    w_sem, own_sem, g_recv, z_send, x_send, y_send, c_send,
    h_send, h_recv, b_send, b_recv,
):
    y = lax.axis_index("dp")
    me = lax.axis_index("expert")
    z = lax.div(me, XS * CS)
    x = lax.rem(lax.div(me, CS), XS)
    c = lax.rem(me, CS)
    n_exp = ZS * XS * CS
    n_dev = 2 * n_exp
    tok, top = idx_ref.shape
    routed, width = acts_ref.shape
    half = width // 2
    model = grad_ref.shape[1]
    lid = y * n_exp + me
    own = slot_of(y, x, z, c)

    def dev(yy, ee):
        return {"dp": yy, "expert": ee}

    barrier = pltpu.get_barrier_semaphore()

    def greet(r, carry):
        other = lax.rem(lid + r, n_dev)
        pl.semaphore_signal(
            barrier, inc=1,
            device_id=dev(lax.div(other, n_exp), lax.rem(other, n_exp)),
            device_id_type=MESH,
        )
        return carry

    lax.fori_loop(1, n_dev, greet, 0)
    w_copy = pltpu.make_async_copy(w_hbm, w_buf, w_sem)
    w_copy.start()
    own_grad = pltpu.make_async_copy(grad_ref, grads.at[own], own_sem.at[0])
    own_grad.start()

    gate = gate_ref[...]
    gate_half = gate.astype(jnp.bfloat16).astype(jnp.float32)
    idx = idx_ref[...].astype(jnp.float32)
    lane = lax.broadcasted_iota(jnp.int32, (tok, routed), 1)
    line = lax.broadcasted_iota(jnp.int32, (tok, routed), 0)
    gate_wide = jnp.zeros((tok, routed), jnp.float32)
    idx_wide = jnp.zeros((tok, routed), jnp.float32)
    for k in range(top):
        here = (lane == line * top + k)
        gate_wide = jnp.where(here, gate_half[:, k:k + 1], gate_wide)
        idx_wide = jnp.where(here, idx[:, k:k + 1], idx_wide)
    gate_row = jnp.sum(gate_wide, axis=0, keepdims=True)
    idx_row = jnp.sum(idx_wide, axis=0, keepdims=True)
    rows = n_exp * tok
    row = lax.broadcasted_iota(jnp.int32, (rows, routed), 0)
    col = lax.broadcasted_iota(jnp.int32, (rows, routed), 1)
    row_exp = lax.div(row, tok).astype(jnp.float32)
    place = jnp.where(
        (idx_row == row_exp) & (lax.div(col, top) == lax.rem(row, tok)), gate_row, 0.0
    ).astype(jnp.bfloat16)
    weighted = jnp.dot(place, acts_ref[...], preferred_element_type=jnp.float32)
    weighted = weighted.astype(jnp.bfloat16).reshape(n_exp, tok, width)
    acts_send[0] = weighted[:, :, :half]
    acts_send[1] = weighted[:, :, half:]

    pl.semaphore_wait(barrier, n_dev - 1)

    def grad_copy(src, slot, sem, yy, ee):
        return pltpu.make_async_remote_copy(
            src_ref=src, dst_ref=grads.at[slot], send_sem=sem, recv_sem=g_recv.at[slot],
            device_id=dev(yy, ee), device_id_type=MESH,
        )

    def arrived(slot):
        grad_copy(grad_ref, slot, c_send.at[0], y, expert_of(x, z, 1 - c)).wait_recv()

    sent = []

    def send(copy, when=None):
        if when is None:
            copy.start()
        else:
            pl.when(when)(copy.start)
        sent.append((when, copy))

    def pass_on(src, yy, xx, zz, to_x, to_y, when=None):
        slot = slot_of(yy, xx, zz, c)
        in_plane = xx * ZS + zz
        if to_x:
            send(grad_copy(src, slot, x_send.at[zz], y, expert_of(1 - x, z, c)), when)
        if to_y:
            send(grad_copy(src, slot, y_send.at[in_plane], 1 - y, me), when)
        send(
            grad_copy(src, slot, c_send.at[yy * XS * ZS + in_plane], y, expert_of(x, z, 1 - c)),
            when,
        )

    def along_z(src, zz, way, when):
        slot = slot_of(y, x, zz, c)
        send(
            grad_copy(
                src, slot, z_send.at[(way + 1) // 2, zz], y, expert_of(x, z + way, c)
            ),
            when,
        )

    for way in (1, -1):
        along_z(grad_ref, z, way, (z + way >= 0) & (z + way < ZS))
    pass_on(grad_ref, y, x, z, True, True)

    def from_z(dist):
        for way in (1, -1):
            zz = z - way * dist
            there = (zz >= 0) & (zz < ZS)
            slot = slot_of(y, x, zz, c)
            pl.when(there)(functools.partial(arrived, slot))
            along_z(grads.at[slot], zz, way, there & (z + way >= 0) & (z + way < ZS))
            pass_on(grads.at[slot], y, x, zz, True, True, there)

    def from_x(dist):
        for way in (1, -1) if dist else (1,):
            zz = z - way * dist
            there = (zz >= 0) & (zz < ZS) if dist else None
            slot = slot_of(y, 1 - x, zz, c)
            if dist:
                pl.when(there)(functools.partial(arrived, slot))
            else:
                arrived(slot)
            pass_on(grads.at[slot], y, 1 - x, zz, False, True, there)

    def acts_copy(r):
        other = lax.rem(lid + r, n_dev)
        yy, ee = lax.div(other, n_exp), lax.rem(other, n_exp)
        return pltpu.make_async_remote_copy(
            src_ref=acts_send.at[yy, ee], dst_ref=acts_in.at[own],
            send_sem=h_send.at[r], recv_sem=h_recv.at[own],
            device_id=dev(yy, ee), device_id_type=MESH,
        )

    def acts_start(r, carry):
        acts_copy(r).start()
        return carry

    own_acts = pltpu.make_async_copy(acts_send.at[y, me], acts_in.at[own], own_sem.at[1])

    def back_copy(slot, zz, xx, cc):
        return pltpu.make_async_remote_copy(
            src_ref=hid.at[slot], dst_ref=back.at[me],
            send_sem=b_send.at[slot], recv_sem=b_recv.at[me],
            device_id=dev(y, expert_of(xx, zz, cc)), device_id_type=MESH,
        )

    per_x = ZS * CS
    tile = 256

    def hidden(xx):
        lhs = grads[pl.ds(slot_of(y, xx, 0, 0), per_x)].reshape(per_x * tok, model)

        @pl.loop(0, width // tile)
        def _(n):
            cols = pl.ds(pl.multiple_of(n * tile, tile), tile)
            part = lax.dot_general(
                lhs, w_buf[cols, :], (((1,), (1,)), ((), ())),
                preferred_element_type=jnp.float32,
            )
            hid[pl.ds(xx * per_x, per_x), :, cols] = part.astype(jnp.bfloat16).reshape(
                per_x, tok, tile
            )

    from_z(1)
    from_x(0)
    from_z(2)
    from_x(1)
    from_z(3)
    lax.fori_loop(1, n_dev, acts_start, 0)
    own_acts.start()
    from_x(2)
    own_grad.wait()
    w_copy.wait()
    for zz in range(ZS):
        arrived(slot_of(y, x, zz, 1 - c))
    hidden(x)
    own_back = pltpu.make_async_copy(hid.at[own - y * n_exp], back.at[me], own_sem.at[2])
    own_back.start()
    for r in range(1, per_x):
        at = lax.rem(z * CS + c + r, per_x)
        back_copy(x * per_x + at, lax.div(at, CS), x, lax.rem(at, CS)).start()
    from_x(3)
    for zz in range(ZS):
        arrived(slot_of(y, 1 - x, zz, 1 - c))
    hidden(1 - x)
    for r in range(per_x):
        at = lax.rem(z * CS + c + r, per_x)
        back_copy((1 - x) * per_x + at, lax.div(at, CS), 1 - x, lax.rem(at, CS)).start()

    for xx in (x, 1 - x):
        for zz in range(ZS):
            slot = slot_of(1 - y, xx, zz, c)
            arrived(slot)
            pass_on(grads.at[slot], 1 - y, xx, zz, False, False)

    def acts_wait(r, carry):
        other = lax.rem(lid + r, n_dev)
        yy, ee = lax.div(other, n_exp), lax.rem(other, n_exp)
        slot = slot_of(
            yy, lax.rem(lax.div(ee, CS), XS), lax.div(ee, XS * CS), lax.rem(ee, CS)
        )
        pltpu.make_async_remote_copy(
            src_ref=acts_send.at[0, 0], dst_ref=acts_in.at[slot],
            send_sem=h_send.at[r], recv_sem=h_recv.at[slot],
            device_id=dev(yy, ee), device_id_type=MESH,
        ).wait_recv()
        return carry

    lax.fori_loop(1, n_dev, acts_wait, 0)
    own_acts.wait()
    acts_t[...] = acts_in[...].reshape(n_dev * tok, half).T
    for xx in range(XS):
        for zz in range(ZS):
            arrived(slot_of(1 - y, xx, zz, 1 - c))

    @pl.loop(0, model // tile)
    def _(n):
        cols = pl.ds(pl.multiple_of(n * tile, tile), tile)
        down_out[:, cols] = jnp.dot(
            acts_t[...], grads[:, :, cols].reshape(n_dev * tok, tile),
            preferred_element_type=jnp.float32,
        ).astype(jnp.bfloat16)

    def back_wait(r, carry):
        ee = lax.rem(me + r, n_exp)
        pltpu.make_async_remote_copy(
            src_ref=hid.at[0], dst_ref=back.at[ee],
            send_sem=b_send.at[0], recv_sem=b_recv.at[ee],
            device_id=dev(y, ee), device_id_type=MESH,
        ).wait_recv()
        return carry

    lax.fori_loop(1, n_exp, back_wait, 0)
    own_back.wait()
    tall_row = lax.broadcasted_iota(jnp.int32, (routed, tok), 0)
    tall_col = lax.broadcasted_iota(jnp.int32, (routed, tok), 1)
    spread = (lax.div(tall_row, top) == tall_col).astype(jnp.float32)
    own_k = (
        lax.broadcasted_iota(jnp.int32, (routed, top), 1)
        == lax.rem(lax.broadcasted_iota(jnp.int32, (routed, top), 0), top)
    ).astype(jnp.float32)
    gate_col = jnp.sum(
        jnp.dot(spread, gate_half, preferred_element_type=jnp.float32) * own_k,
        axis=1, keepdims=True,
    )
    idx_col = jnp.sum(
        jnp.dot(spread, idx, preferred_element_type=jnp.float32) * own_k, axis=1, keepdims=True
    )
    row = lax.broadcasted_iota(jnp.int32, (routed, rows), 0)
    col = lax.broadcasted_iota(jnp.int32, (routed, rows), 1)
    pick = (
        (idx_col == lax.div(col, tok).astype(jnp.float32))
        & (lax.div(row, top) == lax.rem(col, tok))
    ).astype(jnp.float32).astype(jnp.bfloat16)
    picked = jnp.dot(pick, back[...].reshape(rows, width), preferred_element_type=jnp.float32)
    act_out[...] = (gate_col * picked).astype(jnp.bfloat16)
    score = jnp.sum(picked * acts_ref[...].astype(jnp.float32), axis=1, keepdims=True)
    score = score.astype(jnp.bfloat16).astype(jnp.float32)
    gather = (
        lax.div(lane, top) == line
    ).astype(jnp.float32)
    score = jnp.dot(gather, score * own_k, preferred_element_type=jnp.float32)
    logit_out[...] = gate * (score - jnp.sum(gate * score, axis=1, keepdims=True))

    for when, copy in sent:
        if when is None:
            copy.wait_send()
        else:
            pl.when(when)(copy.wait_send)

    def acts_sent(r, carry):
        acts_copy(r).wait_send()
        return carry

    lax.fori_loop(1, n_dev, acts_sent, 0)
    for r in range(1, per_x):
        at = lax.rem(z * CS + c + r, per_x)
        back_copy(x * per_x + at, lax.div(at, CS), x, lax.rem(at, CS)).wait_send()
    for r in range(per_x):
        at = lax.rem(z * CS + c + r, per_x)
        back_copy((1 - x) * per_x + at, lax.div(at, CS), 1 - x, lax.rem(at, CS)).wait_send()


def gathered_shards(out_grad, hidden_acts, gate_weights, expert_idx, down_weight):
    tok, top = expert_idx.shape
    model = out_grad.shape[1]
    width = hidden_acts.shape[2]
    half = width // 2
    n_exp = ZS * XS * CS
    n_dev = 2 * n_exp
    dma = pltpu.SemaphoreType.DMA
    vmem = pl.BlockSpec(memory_space=pltpu.VMEM)
    act, logit, down = pl.pallas_call(
        gather_kernel,
        out_shape=(
            jax.ShapeDtypeStruct((tok * top, width), jnp.bfloat16),
            jax.ShapeDtypeStruct((tok, top), jnp.float32),
            jax.ShapeDtypeStruct((half, model), jnp.bfloat16),
        ),
        in_specs=[vmem] * 4 + [pl.BlockSpec(memory_space=pl.ANY)],
        out_specs=(vmem, vmem, vmem),
        scratch_shapes=[
            pltpu.VMEM((n_dev, tok, model), jnp.bfloat16),
            pltpu.VMEM((width, model), jnp.bfloat16),
            pltpu.VMEM((2, n_exp, tok, half), jnp.bfloat16),
            pltpu.VMEM((n_dev, tok, half), jnp.bfloat16),
            pltpu.VMEM((half, n_dev * tok), jnp.bfloat16),
            pltpu.VMEM((n_exp, tok, width), jnp.bfloat16),
            pltpu.VMEM((n_exp, tok, width), jnp.bfloat16),
            dma,
            dma((3,)),
            dma((n_dev,)),
            dma((2, ZS)),
            dma((ZS,)),
            dma((XS * ZS,)),
            dma((2 * XS * ZS,)),
            dma((n_dev,)),
            dma((n_dev,)),
            dma((n_exp,)),
            dma((n_exp,)),
        ],
        compiler_params=pltpu.CompilerParams(
            collective_id=0, has_side_effects=True, vmem_limit_bytes=48 * 1024 * 1024
        ),
        cost_estimate=pl.CostEstimate(
            flops=6 * n_exp * tok * model * width, bytes_accessed=3 * width * model * 2,
            transcendentals=0,
        ),
    )(
        gate_weights, expert_idx, hidden_acts.reshape(tok * top, width), out_grad,
        down_weight.reshape(width, model),
    )
    return act.reshape(tok, top, width), logit, down[None]


def solution(mesh):
    gathered = mesh.shape["dp"] == 2 and mesh.shape["expert"] == ZS * XS * CS
    return jax.shard_map(
        gathered_shards if gathered else routed_shards,
        mesh=mesh,
        in_specs=(
            P(("dp", "expert"), None),
            P(("dp", "expert"), None, None),
            P(("dp", "expert"), None),
            P(("dp", "expert"), None),
            P("expert", None, None),
        ),
        out_specs=(
            P(("dp", "expert"), None, None),
            P(("dp", "expert"), None),
            P("expert", "dp", None),
        ),
        check_vma=False,
    )
```

```python
import functools

import jax
import jax.numpy as jnp
from jax import lax
from jax.experimental import pallas as pl
from jax.experimental.pallas import tpu as pltpu
from jax.sharding import PartitionSpec as P

MESH = pl.DeviceIdType.MESH
ZS, XS, CS = 4, 2, 2


def routed_shards(out_grad, hidden_acts, gate_weights, expert_idx, down_weight):
    tok_rows, top_count = expert_idx.shape
    routed = tok_rows * top_count
    hidden_width = hidden_acts.shape[2]
    owners = lax.axis_size("expert")
    experts = owners * down_weight.shape[0]
    capacity = min(tok_rows, max(2, (3 * tok_rows * top_count + 2 * experts - 1) // (2 * experts)))
    slot_count = experts * capacity
    flat_expert = expert_idx.reshape(routed)
    member = (flat_expert[:, None] == jnp.arange(experts, dtype=jnp.int32)[None, :]).astype(
        jnp.bfloat16
    )
    row_line = jnp.arange(routed, dtype=jnp.int32)
    earlier_mask = (row_line[:, None] > row_line[None, :]).astype(jnp.bfloat16)
    earlier = jnp.dot(earlier_mask, member, preferred_element_type=jnp.float32)
    position = jnp.sum(earlier * member.astype(jnp.float32), axis=1).astype(jnp.int32)
    slot_index = flat_expert * capacity + position
    placement = (jnp.arange(slot_count, dtype=jnp.int32)[:, None] == slot_index[None, :]).astype(
        jnp.bfloat16
    )
    token_place = jnp.sum(placement.reshape(slot_count, tok_rows, top_count), axis=2)
    gate_half = lax.optimization_barrier(gate_weights.astype(jnp.bfloat16))
    send_grads = jnp.dot(token_place, out_grad, preferred_element_type=jnp.float32).astype(
        jnp.bfloat16
    )
    send_acts = jnp.dot(
        placement, hidden_acts.reshape(routed, hidden_width), preferred_element_type=jnp.float32
    ).astype(jnp.bfloat16)
    send_gate = jnp.dot(
        placement, gate_half.reshape(routed, 1), preferred_element_type=jnp.float32
    ).astype(jnp.bfloat16)
    grads_in, acts_in, gate_in = (
        lax.all_to_all(
            send_grads.reshape(owners, capacity, out_grad.shape[1]),
            "expert",
            split_axis=0,
            concat_axis=0,
            tiled=True,
        ),
        lax.all_to_all(
            send_acts.reshape(owners, capacity, hidden_width),
            "expert",
            split_axis=0,
            concat_axis=0,
            tiled=True,
        ),
        lax.all_to_all(
            send_gate.reshape(owners, capacity), "expert", split_axis=0, concat_axis=0, tiled=True
        ),
    )
    grads_in = grads_in.reshape(slot_count, out_grad.shape[1])
    acts_in = acts_in.reshape(slot_count, hidden_width)
    gate_rows = gate_in.reshape(slot_count, 1).astype(jnp.float32)
    expert_weight = down_weight[0]
    grad_hidden = lax.dot_general(
        grads_in, expert_weight, (((1,), (1,)), ((), ())), preferred_element_type=jnp.float32
    )
    act_back = (gate_rows * grad_hidden).astype(jnp.bfloat16)
    score_back = jnp.sum(grad_hidden * acts_in.astype(jnp.float32), axis=1).astype(jnp.bfloat16)
    scaled_grad = (gate_rows * grads_in.astype(jnp.float32)).astype(jnp.bfloat16)
    back_rows, back_scores = (
        lax.all_to_all(
            act_back.reshape(owners, capacity, hidden_width),
            "expert",
            split_axis=0,
            concat_axis=0,
            tiled=True,
        ),
        lax.all_to_all(
            score_back.reshape(owners, capacity), "expert", split_axis=0, concat_axis=0, tiled=True
        ),
    )
    weight_term = lax.dot_general(
        acts_in, scaled_grad, (((0,), (0,)), ((), ())), preferred_element_type=jnp.float32
    )
    summed = lax.psum_scatter(
        weight_term.astype(jnp.bfloat16), "dp", scatter_dimension=0, tiled=True
    )
    down_grad = summed[None]
    act_grad = lax.dot_general(
        placement,
        back_rows.reshape(slot_count, hidden_width),
        (((0,), (0,)), ((), ())),
        preferred_element_type=jnp.float32,
    ).astype(jnp.bfloat16)
    score_tok = lax.dot_general(
        placement,
        back_scores.reshape(slot_count, 1),
        (((0,), (0,)), ((), ())),
        preferred_element_type=jnp.float32,
    ).reshape(tok_rows, top_count)
    logit_grad = gate_weights * (
        score_tok - jnp.sum(gate_weights * score_tok, axis=1, keepdims=True)
    )
    return (act_grad.reshape(tok_rows, top_count, hidden_width), logit_grad, down_grad)


def slot_of(y, x, z, c):
    return y * (XS * ZS * CS) + x * (ZS * CS) + z * CS + c


def expert_of(x, z, c):
    return z * (XS * CS) + x * CS + c


def gather_kernel(
    gate_hbm, idx_hbm, acts_hbm, grad_ref, w_hbm,
    act_out, logit_out, down_out,
    gate_ref, idx_ref, acts_ref,
    grads, w_buf, acts_send, acts_in, acts_t, hid, back, total, down,
    in_sem, own_sem, out_sem, g_recv, z_send, x_send, y_send, c_send,
    h_send, h_recv, b_send, b_recv,
):
    y = lax.axis_index("dp")
    me = lax.axis_index("expert")
    z = lax.div(me, XS * CS)
    x = lax.rem(lax.div(me, CS), XS)
    c = lax.rem(me, CS)
    n_exp = ZS * XS * CS
    n_dev = 2 * n_exp
    top, tok = idx_ref.shape
    routed, width = acts_ref.shape
    half = width // 2
    model = grad_ref.shape[1]
    lid = y * n_exp + me
    own = slot_of(y, x, z, c)

    def dev(yy, ee):
        return {"dp": yy, "expert": ee}

    barrier = pltpu.get_barrier_semaphore()

    def greet(r, carry):
        other = lax.rem(lid + r, n_dev)
        pl.semaphore_signal(
            barrier, inc=1,
            device_id=dev(lax.div(other, n_exp), lax.rem(other, n_exp)),
            device_id_type=MESH,
        )
        return carry

    lax.fori_loop(1, n_dev, greet, 0)
    own_grad = pltpu.make_async_copy(grad_ref, grads.at[own], own_sem.at[0])
    own_grad.start()
    loads = [
        pltpu.make_async_copy(src, dst, in_sem.at[at])
        for at, (src, dst) in enumerate(
            ((gate_hbm, gate_ref), (idx_hbm, idx_ref), (acts_hbm, acts_ref), (w_hbm, w_buf))
        )
    ]
    for load in loads:
        load.start()
    own_grad.wait()
    pl.semaphore_wait(barrier, n_dev - 1)

    def grad_copy(src, slot, sem, yy, ee):
        return pltpu.make_async_remote_copy(
            src_ref=src, dst_ref=grads.at[slot], send_sem=sem, recv_sem=g_recv.at[slot],
            device_id=dev(yy, ee), device_id_type=MESH,
        )

    def arrived(slot):
        grad_copy(grads.at[slot], slot, c_send.at[0], y, expert_of(x, z, 1 - c)).wait_recv()

    sent = []

    def send(copy, when=None):
        if when is None:
            copy.start()
        else:
            pl.when(when)(copy.start)
        sent.append((when, copy))

    def pass_on(src, yy, xx, zz, to_x, to_y, when=None):
        slot = slot_of(yy, xx, zz, c)
        in_plane = xx * ZS + zz
        if to_x:
            at = zz if yy is y else ZS
            send(grad_copy(src, slot, x_send.at[at], y, expert_of(1 - x, z, c)), when)
        if to_y:
            send(grad_copy(src, slot, y_send.at[in_plane], 1 - y, me), when)
        send(
            grad_copy(src, slot, c_send.at[yy * XS * ZS + in_plane], y, expert_of(x, z, 1 - c)),
            when,
        )

    def along_z(src, zz, way, when):
        slot = slot_of(y, x, zz, c)
        send(
            grad_copy(
                src, slot, z_send.at[(way + 1) // 2, zz], y, expert_of(x, z + way, c)
            ),
            when,
        )

    for way in (1, -1):
        along_z(grads.at[own], z, way, (z + way >= 0) & (z + way < ZS))
    pass_on(grads.at[own], y, x, z, True, True)

    for load in loads[:3]:
        load.wait()
    gate = gate_ref[...]
    gate_half = gate.astype(jnp.bfloat16).astype(jnp.float32)
    idx = idx_ref[...].astype(jnp.float32)
    lane = lax.broadcasted_iota(jnp.int32, (tok, routed), 1)
    line = lax.broadcasted_iota(jnp.int32, (tok, routed), 0)
    widen = (lax.div(lane, top) == line).astype(jnp.float32)
    own_row = lax.broadcasted_iota(jnp.int32, (top, routed), 0) == lax.rem(
        lax.broadcasted_iota(jnp.int32, (top, routed), 1), top
    )
    gate_row = jnp.sum(
        jnp.where(own_row, jnp.dot(gate_half, widen, preferred_element_type=jnp.float32), 0.0),
        axis=0, keepdims=True,
    )
    idx_row = jnp.sum(
        jnp.where(own_row, jnp.dot(idx, widen, preferred_element_type=jnp.float32), 0.0),
        axis=0, keepdims=True,
    )
    rows = n_exp * tok
    row = lax.broadcasted_iota(jnp.int32, (rows, routed), 0)
    col = lax.broadcasted_iota(jnp.int32, (rows, routed), 1)
    row_exp = lax.div(row, tok).astype(jnp.float32)
    place = jnp.where(
        (idx_row == row_exp) & (lax.div(col, top) == lax.rem(row, tok)), gate_row, 0.0
    ).astype(jnp.bfloat16)
    weighted = jnp.dot(place, acts_ref[...], preferred_element_type=jnp.float32)
    weighted = weighted.astype(jnp.bfloat16).reshape(n_exp, tok, width)
    acts_send[0] = weighted[:, :, :half]
    acts_send[1] = weighted[:, :, half:]

    def from_z(dist):
        for way in (1, -1):
            zz = z - way * dist
            there = (zz >= 0) & (zz < ZS)
            slot = slot_of(y, x, zz, c)
            pl.when(there)(functools.partial(arrived, slot))
            along_z(grads.at[slot], zz, way, there & (z + way >= 0) & (z + way < ZS))
            pass_on(grads.at[slot], y, x, zz, True, True, there)

    def from_x(dist):
        for way in (1, -1) if dist else (1,):
            zz = z - way * dist
            there = (zz >= 0) & (zz < ZS) if dist else None
            slot = slot_of(y, 1 - x, zz, c)
            if dist:
                pl.when(there)(functools.partial(arrived, slot))
            else:
                arrived(slot)
            pass_on(grads.at[slot], y, 1 - x, zz, False, dist != 2, there)

    def acts_copy(r):
        other = lax.rem(lid + r, n_dev)
        yy, ee = lax.div(other, n_exp), lax.rem(other, n_exp)
        return pltpu.make_async_remote_copy(
            src_ref=acts_send.at[yy, ee], dst_ref=acts_in.at[own],
            send_sem=h_send.at[r], recv_sem=h_recv.at[own],
            device_id=dev(yy, ee), device_id_type=MESH,
        )

    def acts_start(r, carry):
        acts_copy(r).start()
        return carry

    own_acts = pltpu.make_async_copy(acts_send.at[y, me], acts_in.at[own], own_sem.at[1])

    def back_copy(slot, zz, xx, cc):
        return pltpu.make_async_remote_copy(
            src_ref=hid.at[slot], dst_ref=back.at[me],
            send_sem=b_send.at[slot], recv_sem=b_recv.at[me],
            device_id=dev(y, expert_of(xx, zz, cc)), device_id_type=MESH,
        )

    per_x = ZS * CS
    tile = 256

    def hidden(xx):
        lhs = grads[pl.ds(slot_of(y, xx, 0, 0), per_x)].reshape(per_x * tok, model)

        @pl.loop(0, width // tile)
        def _(n):
            cols = pl.ds(pl.multiple_of(n * tile, tile), tile)
            part = lax.dot_general(
                lhs, w_buf[cols, :], (((1,), (1,)), ((), ())),
                preferred_element_type=jnp.float32,
            )
            hid[pl.ds(xx * per_x, per_x), :, cols] = part.astype(jnp.bfloat16).reshape(
                per_x, tok, tile
            )

    from_z(1)
    from_x(0)
    from_z(2)
    from_x(1)
    from_z(3)
    lax.fori_loop(1, n_dev, acts_start, 0)
    own_acts.start()
    from_x(2)
    loads[3].wait()
    for zz in range(ZS):
        arrived(slot_of(y, x, zz, 1 - c))
    hidden(x)
    own_back = pltpu.make_async_copy(hid.at[own - y * n_exp], back.at[me], own_sem.at[2])
    own_back.start()
    for r in range(1, per_x):
        at = lax.rem(z * CS + c + r, per_x)
        back_copy(x * per_x + at, lax.div(at, CS), x, lax.rem(at, CS)).start()
    from_x(3)
    for zz in range(ZS):
        arrived(slot_of(y, 1 - x, zz, 1 - c))
    hidden(1 - x)
    for r in range(per_x):
        at = lax.rem(z * CS + c + r, per_x)
        back_copy((1 - x) * per_x + at, lax.div(at, CS), 1 - x, lax.rem(at, CS)).start()

    def from_group(xx, dist, to_x):
        for way in (1, -1) if dist else (1,):
            zz = z - way * dist
            there = (zz >= 0) & (zz < ZS) if dist else None
            slot = slot_of(1 - y, xx, zz, c)
            if dist:
                pl.when(there)(functools.partial(arrived, slot))
            else:
                arrived(slot)
            pass_on(grads.at[slot], 1 - y, xx, zz, to_x, False, there)

    def acts_wait(r, group):
        ee = lax.rem(me + r, n_exp)
        slot = slot_of(
            group, lax.rem(lax.div(ee, CS), XS), lax.div(ee, XS * CS), lax.rem(ee, CS)
        )
        pltpu.make_async_remote_copy(
            src_ref=acts_send.at[0, 0], dst_ref=acts_in.at[slot],
            send_sem=h_send.at[0], recv_sem=h_recv.at[slot],
            device_id=dev(1 - y, me), device_id_type=MESH,
        ).wait_recv()
        return group

    def turn(group, at):
        rows_in = acts_in[pl.ds(group * n_exp, n_exp)].reshape(n_exp * tok, half)
        acts_t[at] = rows_in.T

    def down_part(group, at, cols):
        return jnp.dot(
            acts_t[at], grads[pl.ds(group * n_exp, n_exp), :, cols].reshape(n_exp * tok, tile),
            preferred_element_type=jnp.float32,
        )

    for dist in range(ZS):
        from_group(x, dist, dist == 2)

    lax.fori_loop(1, n_exp, acts_wait, y)
    own_acts.wait()
    turn(y, 0)

    @pl.loop(0, model // tile)
    def _(n):
        cols = pl.ds(pl.multiple_of(n * tile, tile), tile)
        total[:, cols] = down_part(y, 0, cols)

    for dist in range(ZS):
        from_group(1 - x, dist, False)

    def back_wait(r, carry):
        ee = lax.rem(me + r, n_exp)
        pltpu.make_async_remote_copy(
            src_ref=hid.at[0], dst_ref=back.at[ee],
            send_sem=b_send.at[0], recv_sem=b_recv.at[ee],
            device_id=dev(1 - y, me), device_id_type=MESH,
        ).wait_recv()
        return carry

    lax.fori_loop(1, n_exp, back_wait, 0)
    own_back.wait()
    tall_row = lax.broadcasted_iota(jnp.int32, (routed, tok), 0)
    tall_col = lax.broadcasted_iota(jnp.int32, (routed, tok), 1)
    spread = (lax.div(tall_row, top) == tall_col).astype(jnp.float32)
    own_k = (
        lax.broadcasted_iota(jnp.int32, (routed, top), 1)
        == lax.rem(lax.broadcasted_iota(jnp.int32, (routed, top), 0), top)
    ).astype(jnp.float32)

    def column(of):
        wide = lax.dot_general(
            spread, of, (((1,), (1,)), ((), ())), preferred_element_type=jnp.float32
        )
        return jnp.sum(wide * own_k, axis=1, keepdims=True)

    gate_col = column(gate_half)
    idx_col = column(idx)
    row = lax.broadcasted_iota(jnp.int32, (routed, rows), 0)
    col = lax.broadcasted_iota(jnp.int32, (routed, rows), 1)
    pick = (
        (idx_col == lax.div(col, tok).astype(jnp.float32))
        & (lax.div(row, top) == lax.rem(col, tok))
    ).astype(jnp.float32).astype(jnp.bfloat16)
    picked = jnp.dot(pick, back[...].reshape(rows, width), preferred_element_type=jnp.float32)
    act_out[...] = (gate_col * picked).astype(jnp.bfloat16)
    score = jnp.sum(picked * acts_ref[...].astype(jnp.float32), axis=1, keepdims=True)
    score = score.astype(jnp.bfloat16).astype(jnp.float32)
    score = jnp.dot(own_row.astype(jnp.float32), score * spread, preferred_element_type=jnp.float32)
    logit_out[...] = gate * (score - jnp.sum(gate * score, axis=0, keepdims=True))

    lax.fori_loop(0, n_exp, acts_wait, 1 - y)
    turn(1 - y, 1)
    for xx in (x, 1 - x):
        for zz in range(ZS):
            arrived(slot_of(1 - y, xx, zz, 1 - c))

    def down_copy(n):
        cols = pl.ds(pl.multiple_of(n * tile, tile), tile)
        return pltpu.make_async_copy(down.at[:, cols], down_out.at[:, cols], out_sem.at[n])

    @pl.loop(0, model // tile)
    def _(n):
        cols = pl.ds(pl.multiple_of(n * tile, tile), tile)
        down[:, cols] = (total[:, cols] + down_part(1 - y, 1, cols)).astype(jnp.bfloat16)
        down_copy(n).start()

    for when, copy in sent:
        if when is None:
            copy.wait_send()
        else:
            pl.when(when)(copy.wait_send)

    def acts_sent(r, carry):
        acts_copy(r).wait_send()
        return carry

    lax.fori_loop(1, n_dev, acts_sent, 0)
    for r in range(1, per_x):
        at = lax.rem(z * CS + c + r, per_x)
        back_copy(x * per_x + at, lax.div(at, CS), x, lax.rem(at, CS)).wait_send()
    for r in range(per_x):
        at = lax.rem(z * CS + c + r, per_x)
        back_copy((1 - x) * per_x + at, lax.div(at, CS), 1 - x, lax.rem(at, CS)).wait_send()

    @pl.loop(0, model // tile)
    def _(n):
        down_copy(n).wait()


def gathered_shards(out_grad, hidden_acts, gate_weights, expert_idx, down_weight):
    tok, top = expert_idx.shape
    model = out_grad.shape[1]
    width = hidden_acts.shape[2]
    half = width // 2
    n_exp = ZS * XS * CS
    n_dev = 2 * n_exp
    dma = pltpu.SemaphoreType.DMA
    vmem = pl.BlockSpec(memory_space=pltpu.VMEM)
    hbm = pl.BlockSpec(memory_space=pltpu.HBM)
    act, logit, down = pl.pallas_call(
        gather_kernel,
        out_shape=(
            jax.ShapeDtypeStruct((tok * top, width), jnp.bfloat16),
            jax.ShapeDtypeStruct((top, tok), jnp.float32),
            jax.ShapeDtypeStruct((half, model), jnp.bfloat16),
        ),
        in_specs=[hbm] * 5,
        out_specs=(vmem, vmem, hbm),
        scratch_shapes=[
            pltpu.VMEM((top, tok), jnp.float32),
            pltpu.VMEM((top, tok), jnp.int32),
            pltpu.VMEM((tok * top, width), jnp.bfloat16),
            pltpu.VMEM((n_dev, tok, model), jnp.bfloat16),
            pltpu.VMEM((width, model), jnp.bfloat16),
            pltpu.VMEM((2, n_exp, tok, half), jnp.bfloat16),
            pltpu.VMEM((n_dev, tok, half), jnp.bfloat16),
            pltpu.VMEM((2, half, n_exp * tok), jnp.bfloat16),
            pltpu.VMEM((n_exp, tok, width), jnp.bfloat16),
            pltpu.VMEM((n_exp, tok, width), jnp.bfloat16),
            pltpu.VMEM((half, model), jnp.float32),
            pltpu.VMEM((half, model), jnp.bfloat16),
            dma((4,)),
            dma((3,)),
            dma((model // 256,)),
            dma((n_dev,)),
            dma((2, ZS)),
            dma((ZS + 1,)),
            dma((XS * ZS,)),
            dma((2 * XS * ZS,)),
            dma((n_dev,)),
            dma((n_dev,)),
            dma((n_exp,)),
            dma((n_exp,)),
        ],
        compiler_params=pltpu.CompilerParams(
            collective_id=0, has_side_effects=True, vmem_limit_bytes=56 * 1024 * 1024
        ),
        cost_estimate=pl.CostEstimate(
            flops=6 * n_exp * tok * model * width, bytes_accessed=3 * width * model * 2,
            transcendentals=0,
        ),
    )(
        gate_weights.T, expert_idx.T, hidden_acts.reshape(tok * top, width), out_grad,
        down_weight.reshape(width, model),
    )
    return act.reshape(tok, top, width), logit.T, down[None]


def solution(mesh):
    gathered = mesh.shape["dp"] == 2 and mesh.shape["expert"] == ZS * XS * CS
    return jax.shard_map(
        gathered_shards if gathered else routed_shards,
        mesh=mesh,
        in_specs=(
            P(("dp", "expert"), None),
            P(("dp", "expert"), None, None),
            P(("dp", "expert"), None),
            P(("dp", "expert"), None),
            P("expert", None, None),
        ),
        out_specs=(
            P(("dp", "expert"), None, None),
            P(("dp", "expert"), None),
            P("expert", "dp", None),
        ),
        check_vma=False,
    )
```

```python
import functools

import jax
import jax.numpy as jnp
from jax import lax
from jax.experimental import pallas as pl
from jax.experimental.pallas import tpu as pltpu
from jax.sharding import PartitionSpec as P

MESH = pl.DeviceIdType.MESH
ZS, XS, CS = 4, 2, 2


def routed_shards(out_grad, hidden_acts, gate_weights, expert_idx, down_weight):
    tok_rows, top_count = expert_idx.shape
    routed = tok_rows * top_count
    hidden_width = hidden_acts.shape[2]
    owners = lax.axis_size("expert")
    experts = owners * down_weight.shape[0]
    capacity = min(tok_rows, max(2, (3 * tok_rows * top_count + 2 * experts - 1) // (2 * experts)))
    slot_count = experts * capacity
    flat_expert = expert_idx.reshape(routed)
    member = (flat_expert[:, None] == jnp.arange(experts, dtype=jnp.int32)[None, :]).astype(
        jnp.bfloat16
    )
    row_line = jnp.arange(routed, dtype=jnp.int32)
    earlier_mask = (row_line[:, None] > row_line[None, :]).astype(jnp.bfloat16)
    earlier = jnp.dot(earlier_mask, member, preferred_element_type=jnp.float32)
    position = jnp.sum(earlier * member.astype(jnp.float32), axis=1).astype(jnp.int32)
    slot_index = flat_expert * capacity + position
    placement = (jnp.arange(slot_count, dtype=jnp.int32)[:, None] == slot_index[None, :]).astype(
        jnp.bfloat16
    )
    token_place = jnp.sum(placement.reshape(slot_count, tok_rows, top_count), axis=2)
    gate_half = lax.optimization_barrier(gate_weights.astype(jnp.bfloat16))
    send_grads = jnp.dot(token_place, out_grad, preferred_element_type=jnp.float32).astype(
        jnp.bfloat16
    )
    send_acts = jnp.dot(
        placement, hidden_acts.reshape(routed, hidden_width), preferred_element_type=jnp.float32
    ).astype(jnp.bfloat16)
    send_gate = jnp.dot(
        placement, gate_half.reshape(routed, 1), preferred_element_type=jnp.float32
    ).astype(jnp.bfloat16)
    grads_in, acts_in, gate_in = (
        lax.all_to_all(
            send_grads.reshape(owners, capacity, out_grad.shape[1]),
            "expert",
            split_axis=0,
            concat_axis=0,
            tiled=True,
        ),
        lax.all_to_all(
            send_acts.reshape(owners, capacity, hidden_width),
            "expert",
            split_axis=0,
            concat_axis=0,
            tiled=True,
        ),
        lax.all_to_all(
            send_gate.reshape(owners, capacity), "expert", split_axis=0, concat_axis=0, tiled=True
        ),
    )
    grads_in = grads_in.reshape(slot_count, out_grad.shape[1])
    acts_in = acts_in.reshape(slot_count, hidden_width)
    gate_rows = gate_in.reshape(slot_count, 1).astype(jnp.float32)
    expert_weight = down_weight[0]
    grad_hidden = lax.dot_general(
        grads_in, expert_weight, (((1,), (1,)), ((), ())), preferred_element_type=jnp.float32
    )
    act_back = (gate_rows * grad_hidden).astype(jnp.bfloat16)
    score_back = jnp.sum(grad_hidden * acts_in.astype(jnp.float32), axis=1).astype(jnp.bfloat16)
    scaled_grad = (gate_rows * grads_in.astype(jnp.float32)).astype(jnp.bfloat16)
    back_rows, back_scores = (
        lax.all_to_all(
            act_back.reshape(owners, capacity, hidden_width),
            "expert",
            split_axis=0,
            concat_axis=0,
            tiled=True,
        ),
        lax.all_to_all(
            score_back.reshape(owners, capacity), "expert", split_axis=0, concat_axis=0, tiled=True
        ),
    )
    weight_term = lax.dot_general(
        acts_in, scaled_grad, (((0,), (0,)), ((), ())), preferred_element_type=jnp.float32
    )
    summed = lax.psum_scatter(
        weight_term.astype(jnp.bfloat16), "dp", scatter_dimension=0, tiled=True
    )
    down_grad = summed[None]
    act_grad = lax.dot_general(
        placement,
        back_rows.reshape(slot_count, hidden_width),
        (((0,), (0,)), ((), ())),
        preferred_element_type=jnp.float32,
    ).astype(jnp.bfloat16)
    score_tok = lax.dot_general(
        placement,
        back_scores.reshape(slot_count, 1),
        (((0,), (0,)), ((), ())),
        preferred_element_type=jnp.float32,
    ).reshape(tok_rows, top_count)
    logit_grad = gate_weights * (
        score_tok - jnp.sum(gate_weights * score_tok, axis=1, keepdims=True)
    )
    return (act_grad.reshape(tok_rows, top_count, hidden_width), logit_grad, down_grad)


def slot_of(y, x, z, c):
    return y * (XS * ZS * CS) + x * (ZS * CS) + z * CS + c


def expert_of(x, z, c):
    return z * (XS * CS) + x * CS + c


def gather_kernel(
    gate_hbm, idx_hbm, acts_hbm, grad_ref, w_hbm,
    act_out, logit_out, down_out,
    gate_ref, idx_ref, acts_ref,
    grads, w_buf, acts_send, acts_in, acts_t, hid, back, total,
    in_sem, own_sem, g_recv, z_send, x_send, y_send, c_send,
    h_send, h_recv, b_send, b_recv,
):
    y = lax.axis_index("dp")
    me = lax.axis_index("expert")
    z = lax.div(me, XS * CS)
    x = lax.rem(lax.div(me, CS), XS)
    c = lax.rem(me, CS)
    n_exp = ZS * XS * CS
    n_dev = 2 * n_exp
    top, tok = idx_ref.shape
    routed, width = acts_ref.shape
    half = width // 2
    model = grad_ref.shape[1]
    lid = y * n_exp + me
    own = slot_of(y, x, z, c)

    def dev(yy, ee):
        return {"dp": yy, "expert": ee}

    barrier = pltpu.get_barrier_semaphore()

    def greet(r, carry):
        other = lax.rem(lid + r, n_dev)
        pl.semaphore_signal(
            barrier, inc=1,
            device_id=dev(lax.div(other, n_exp), lax.rem(other, n_exp)),
            device_id_type=MESH,
        )
        return carry

    lax.fori_loop(1, n_dev, greet, 0)
    own_grad = pltpu.make_async_copy(grad_ref, grads.at[own], own_sem.at[0])
    own_grad.start()
    loads = [
        pltpu.make_async_copy(src, dst, in_sem.at[at])
        for at, (src, dst) in enumerate(
            ((gate_hbm, gate_ref), (idx_hbm, idx_ref), (acts_hbm, acts_ref), (w_hbm, w_buf))
        )
    ]
    for load in loads:
        load.start()
    own_grad.wait()
    pl.semaphore_wait(barrier, n_dev - 1)

    def grad_copy(src, slot, sem, yy, ee):
        return pltpu.make_async_remote_copy(
            src_ref=src, dst_ref=grads.at[slot], send_sem=sem, recv_sem=g_recv.at[slot],
            device_id=dev(yy, ee), device_id_type=MESH,
        )

    def arrived(slot):
        grad_copy(grads.at[slot], slot, c_send.at[0], y, expert_of(x, z, 1 - c)).wait_recv()

    sent = []

    def send(copy, when=None):
        if when is None:
            copy.start()
        else:
            pl.when(when)(copy.start)
        sent.append((when, copy))

    def pass_on(src, yy, xx, zz, to_x, to_y, when=None):
        slot = slot_of(yy, xx, zz, c)
        in_plane = xx * ZS + zz
        if to_x:
            at = zz if yy is y else ZS
            send(grad_copy(src, slot, x_send.at[at], y, expert_of(1 - x, z, c)), when)
        if to_y:
            send(grad_copy(src, slot, y_send.at[in_plane], 1 - y, me), when)
        send(
            grad_copy(src, slot, c_send.at[yy * XS * ZS + in_plane], y, expert_of(x, z, 1 - c)),
            when,
        )

    def along_z(src, zz, way, when):
        slot = slot_of(y, x, zz, c)
        send(
            grad_copy(
                src, slot, z_send.at[(way + 1) // 2, zz], y, expert_of(x, z + way, c)
            ),
            when,
        )

    for way in (1, -1):
        along_z(grads.at[own], z, way, (z + way >= 0) & (z + way < ZS))
    pass_on(grads.at[own], y, x, z, True, True)

    for load in loads[:3]:
        load.wait()
    gate = gate_ref[...]
    gate_half = gate.astype(jnp.bfloat16).astype(jnp.float32)
    idx = idx_ref[...].astype(jnp.float32)
    lane = lax.broadcasted_iota(jnp.int32, (tok, routed), 1)
    line = lax.broadcasted_iota(jnp.int32, (tok, routed), 0)
    widen = (lax.div(lane, top) == line).astype(jnp.float32)
    own_row = lax.broadcasted_iota(jnp.int32, (top, routed), 0) == lax.rem(
        lax.broadcasted_iota(jnp.int32, (top, routed), 1), top
    )
    gate_row = jnp.sum(
        jnp.where(own_row, jnp.dot(gate_half, widen, preferred_element_type=jnp.float32), 0.0),
        axis=0, keepdims=True,
    )
    idx_row = jnp.sum(
        jnp.where(own_row, jnp.dot(idx, widen, preferred_element_type=jnp.float32), 0.0),
        axis=0, keepdims=True,
    )
    rows = n_exp * tok
    row = lax.broadcasted_iota(jnp.int32, (rows, routed), 0)
    col = lax.broadcasted_iota(jnp.int32, (rows, routed), 1)
    row_exp = lax.div(row, tok).astype(jnp.float32)
    place = jnp.where(
        (idx_row == row_exp) & (lax.div(col, top) == lax.rem(row, tok)), gate_row, 0.0
    ).astype(jnp.bfloat16)
    weighted = jnp.dot(place, acts_ref[...], preferred_element_type=jnp.float32)
    weighted = weighted.astype(jnp.bfloat16).reshape(n_exp, tok, width)
    acts_send[0] = weighted[:, :, :half]
    acts_send[1] = weighted[:, :, half:]

    tall_row = lax.broadcasted_iota(jnp.int32, (routed, tok), 0)
    tall_col = lax.broadcasted_iota(jnp.int32, (routed, tok), 1)
    spread = (lax.div(tall_row, top) == tall_col).astype(jnp.float32)
    own_k = (
        lax.broadcasted_iota(jnp.int32, (routed, top), 1)
        == lax.rem(lax.broadcasted_iota(jnp.int32, (routed, top), 0), top)
    ).astype(jnp.float32)

    def column(of):
        wide = lax.dot_general(
            spread, of, (((1,), (1,)), ((), ())), preferred_element_type=jnp.float32
        )
        return jnp.sum(wide * own_k, axis=1, keepdims=True)

    gate_col = column(gate_half)
    idx_col = column(idx)
    row = lax.broadcasted_iota(jnp.int32, (routed, rows), 0)
    col = lax.broadcasted_iota(jnp.int32, (routed, rows), 1)
    pick = (
        (idx_col == lax.div(col, tok).astype(jnp.float32))
        & (lax.div(row, top) == lax.rem(col, tok))
    ).astype(jnp.float32).astype(jnp.bfloat16)

    def from_z(dist):
        for way in (1, -1):
            zz = z - way * dist
            there = (zz >= 0) & (zz < ZS)
            slot = slot_of(y, x, zz, c)
            pl.when(there)(functools.partial(arrived, slot))
            along_z(grads.at[slot], zz, way, there & (z + way >= 0) & (z + way < ZS))
            pass_on(grads.at[slot], y, x, zz, True, True, there)

    def from_x(dist):
        for way in (1, -1) if dist else (1,):
            zz = z - way * dist
            there = (zz >= 0) & (zz < ZS) if dist else None
            slot = slot_of(y, 1 - x, zz, c)
            if dist:
                pl.when(there)(functools.partial(arrived, slot))
            else:
                arrived(slot)
            pass_on(grads.at[slot], y, 1 - x, zz, False, dist != 2, there)

    def acts_copy(r):
        other = lax.rem(lid + r, n_dev)
        yy, ee = lax.div(other, n_exp), lax.rem(other, n_exp)
        return pltpu.make_async_remote_copy(
            src_ref=acts_send.at[yy, ee], dst_ref=acts_in.at[own],
            send_sem=h_send.at[r], recv_sem=h_recv.at[own],
            device_id=dev(yy, ee), device_id_type=MESH,
        )

    def acts_start(r, carry):
        acts_copy(r).start()
        return carry

    own_acts = pltpu.make_async_copy(acts_send.at[y, me], acts_in.at[own], own_sem.at[1])

    def back_copy(slot, zz, xx, cc):
        return pltpu.make_async_remote_copy(
            src_ref=hid.at[slot], dst_ref=back.at[me],
            send_sem=b_send.at[slot], recv_sem=b_recv.at[me],
            device_id=dev(y, expert_of(xx, zz, cc)), device_id_type=MESH,
        )

    per_x = ZS * CS
    tile = model // 4

    def hidden():
        part = lax.dot_general(
            grads[pl.ds(y * n_exp, n_exp)].reshape(n_exp * tok, model), w_buf[...],
            (((1,), (1,)), ((), ())), preferred_element_type=jnp.float32,
        )
        hid[...] = part.astype(jnp.bfloat16).reshape(n_exp, tok, width)

    def from_group(xx, dist, to_x):
        for way in (1, -1) if dist else (1,):
            zz = z - way * dist
            there = (zz >= 0) & (zz < ZS) if dist else None
            slot = slot_of(1 - y, xx, zz, c)
            if dist:
                pl.when(there)(functools.partial(arrived, slot))
            else:
                arrived(slot)
            pass_on(grads.at[slot], 1 - y, xx, zz, to_x, False, there)

    from_z(1)
    from_x(0)
    from_z(2)
    from_x(1)
    from_z(3)
    lax.fori_loop(1, n_dev, acts_start, 0)
    own_acts.start()
    from_x(2)
    from_x(3)
    for dist in range(2):
        from_group(x, dist, False)
    loads[3].wait()
    for xx in (x, 1 - x):
        for zz in range(ZS):
            arrived(slot_of(y, xx, zz, 1 - c))
    hidden()
    own_back = pltpu.make_async_copy(hid.at[own - y * n_exp], back.at[me], own_sem.at[2])
    own_back.start()

    def each_back():
        for xx in (1 - x, x):
            for r in range(per_x):
                at = lax.rem(z * CS + c + r, per_x)
                if xx is not x or r:
                    yield back_copy(xx * per_x + at, lax.div(at, CS), xx, lax.rem(at, CS))

    for copy in each_back():
        copy.start()

    def acts_wait(r, group):
        ee = lax.rem(me + r, n_exp)
        slot = slot_of(
            group, lax.rem(lax.div(ee, CS), XS), lax.div(ee, XS * CS), lax.rem(ee, CS)
        )
        pltpu.make_async_remote_copy(
            src_ref=acts_send.at[0, 0], dst_ref=acts_in.at[slot],
            send_sem=h_send.at[0], recv_sem=h_recv.at[slot],
            device_id=dev(1 - y, me), device_id_type=MESH,
        ).wait_recv()
        return group

    def turn(group, at):
        rows_in = acts_in[pl.ds(group * n_exp, n_exp)].reshape(n_exp * tok, half)
        acts_t[at] = rows_in.T

    def down_part(group, at, cols):
        return jnp.dot(
            acts_t[at], grads[pl.ds(group * n_exp, n_exp), :, cols].reshape(n_exp * tok, tile),
            preferred_element_type=jnp.float32,
        )

    for dist in range(2, ZS):
        from_group(x, dist, dist == 2)

    lax.fori_loop(1, n_exp, acts_wait, y)
    own_acts.wait()
    turn(y, 0)

    @pl.loop(0, model // tile)
    def _(n):
        cols = pl.ds(pl.multiple_of(n * tile, tile), tile)
        total[:, cols] = down_part(y, 0, cols)

    for dist in range(ZS):
        from_group(1 - x, dist, False)

    def back_wait(r, carry):
        ee = lax.rem(me + r, n_exp)
        pltpu.make_async_remote_copy(
            src_ref=hid.at[0], dst_ref=back.at[ee],
            send_sem=b_send.at[0], recv_sem=b_recv.at[ee],
            device_id=dev(1 - y, me), device_id_type=MESH,
        ).wait_recv()
        return carry

    lax.fori_loop(1, n_exp, back_wait, 0)
    own_back.wait()
    picked = jnp.dot(pick, back[...].reshape(rows, width), preferred_element_type=jnp.float32)
    act_out[...] = (gate_col * picked).astype(jnp.bfloat16)
    score = jnp.sum(picked * acts_ref[...].astype(jnp.float32), axis=1, keepdims=True)
    score = score.astype(jnp.bfloat16).astype(jnp.float32)
    score = jnp.dot(own_row.astype(jnp.float32), score * spread, preferred_element_type=jnp.float32)
    logit_out[...] = gate * (score - jnp.sum(gate * score, axis=0, keepdims=True))

    lax.fori_loop(0, n_exp, acts_wait, 1 - y)
    turn(1 - y, 1)
    for xx in (x, 1 - x):
        for zz in range(ZS):
            arrived(slot_of(1 - y, xx, zz, 1 - c))

    @pl.loop(0, model // tile)
    def _(n):
        cols = pl.ds(pl.multiple_of(n * tile, tile), tile)
        down_out[:, cols] = (total[:, cols] + down_part(1 - y, 1, cols)).astype(jnp.bfloat16)

    for when, copy in sent:
        if when is None:
            copy.wait_send()
        else:
            pl.when(when)(copy.wait_send)

    def acts_sent(r, carry):
        acts_copy(r).wait_send()
        return carry

    lax.fori_loop(1, n_dev, acts_sent, 0)
    for copy in each_back():
        copy.wait_send()


def gathered_shards(out_grad, hidden_acts, gate_weights, expert_idx, down_weight):
    tok, top = expert_idx.shape
    model = out_grad.shape[1]
    width = hidden_acts.shape[2]
    half = width // 2
    n_exp = ZS * XS * CS
    n_dev = 2 * n_exp
    dma = pltpu.SemaphoreType.DMA
    vmem = pl.BlockSpec(memory_space=pltpu.VMEM)
    hbm = pl.BlockSpec(memory_space=pltpu.HBM)
    act, logit, down = pl.pallas_call(
        gather_kernel,
        out_shape=(
            jax.ShapeDtypeStruct((tok * top, width), jnp.bfloat16),
            jax.ShapeDtypeStruct((top, tok), jnp.float32),
            jax.ShapeDtypeStruct((half, model), jnp.bfloat16),
        ),
        in_specs=[hbm] * 5,
        out_specs=(vmem, vmem, vmem),
        scratch_shapes=[
            pltpu.VMEM((top, tok), jnp.float32),
            pltpu.VMEM((top, tok), jnp.int32),
            pltpu.VMEM((tok * top, width), jnp.bfloat16),
            pltpu.VMEM((n_dev, tok, model), jnp.bfloat16),
            pltpu.VMEM((width, model), jnp.bfloat16),
            pltpu.VMEM((2, n_exp, tok, half), jnp.bfloat16),
            pltpu.VMEM((n_dev, tok, half), jnp.bfloat16),
            pltpu.VMEM((2, half, n_exp * tok), jnp.bfloat16),
            pltpu.VMEM((n_exp, tok, width), jnp.bfloat16),
            pltpu.VMEM((n_exp, tok, width), jnp.bfloat16),
            pltpu.VMEM((half, model), jnp.float32),
            dma((4,)),
            dma((3,)),
            dma((n_dev,)),
            dma((2, ZS)),
            dma((ZS + 1,)),
            dma((XS * ZS,)),
            dma((2 * XS * ZS,)),
            dma((n_dev,)),
            dma((n_dev,)),
            dma((n_exp,)),
            dma((n_exp,)),
        ],
        compiler_params=pltpu.CompilerParams(
            collective_id=0, has_side_effects=True, vmem_limit_bytes=36 * 1024 * 1024
        ),
        cost_estimate=pl.CostEstimate(
            flops=6 * n_exp * tok * model * width, bytes_accessed=3 * width * model * 2,
            transcendentals=0,
        ),
    )(
        *(
            pltpu.with_memory_space_constraint(array, pltpu.HBM)
            for array in (
                gate_weights.T, expert_idx.T, hidden_acts.reshape(tok * top, width), out_grad,
                down_weight.reshape(width, model),
            )
        )
    )
    return act.reshape(tok, top, width), logit.T, down[None]


def solution(mesh):
    gathered = mesh.shape["dp"] == 2 and mesh.shape["expert"] == ZS * XS * CS
    return jax.shard_map(
        gathered_shards if gathered else routed_shards,
        mesh=mesh,
        in_specs=(
            P(("dp", "expert"), None),
            P(("dp", "expert"), None, None),
            P(("dp", "expert"), None),
            P(("dp", "expert"), None),
            P("expert", None, None),
        ),
        out_specs=(
            P(("dp", "expert"), None, None),
            P(("dp", "expert"), None),
            P("expert", "dp", None),
        ),
        check_vma=False,
    )
```

```python
import functools

import jax
import jax.numpy as jnp
from jax import lax
from jax.experimental import pallas as pl
from jax.experimental.pallas import tpu as pltpu
from jax.sharding import PartitionSpec as P

MESH = pl.DeviceIdType.MESH
ZS, XS, CS = 4, 2, 2
PARTS = 2


def routed_shards(out_grad, hidden_acts, gate_weights, expert_idx, down_weight):
    tok_rows, top_count = expert_idx.shape
    routed = tok_rows * top_count
    hidden_width = hidden_acts.shape[2]
    owners = lax.axis_size("expert")
    experts = owners * down_weight.shape[0]
    capacity = min(tok_rows, max(2, (3 * tok_rows * top_count + 2 * experts - 1) // (2 * experts)))
    slot_count = experts * capacity
    flat_expert = expert_idx.reshape(routed)
    member = (flat_expert[:, None] == jnp.arange(experts, dtype=jnp.int32)[None, :]).astype(
        jnp.bfloat16
    )
    row_line = jnp.arange(routed, dtype=jnp.int32)
    earlier_mask = (row_line[:, None] > row_line[None, :]).astype(jnp.bfloat16)
    earlier = jnp.dot(earlier_mask, member, preferred_element_type=jnp.float32)
    position = jnp.sum(earlier * member.astype(jnp.float32), axis=1).astype(jnp.int32)
    slot_index = flat_expert * capacity + position
    placement = (jnp.arange(slot_count, dtype=jnp.int32)[:, None] == slot_index[None, :]).astype(
        jnp.bfloat16
    )
    token_place = jnp.sum(placement.reshape(slot_count, tok_rows, top_count), axis=2)
    gate_half = lax.optimization_barrier(gate_weights.astype(jnp.bfloat16))
    send_grads = jnp.dot(token_place, out_grad, preferred_element_type=jnp.float32).astype(
        jnp.bfloat16
    )
    send_acts = jnp.dot(
        placement, hidden_acts.reshape(routed, hidden_width), preferred_element_type=jnp.float32
    ).astype(jnp.bfloat16)
    send_gate = jnp.dot(
        placement, gate_half.reshape(routed, 1), preferred_element_type=jnp.float32
    ).astype(jnp.bfloat16)
    grads_in, acts_in, gate_in = (
        lax.all_to_all(
            send_grads.reshape(owners, capacity, out_grad.shape[1]),
            "expert",
            split_axis=0,
            concat_axis=0,
            tiled=True,
        ),
        lax.all_to_all(
            send_acts.reshape(owners, capacity, hidden_width),
            "expert",
            split_axis=0,
            concat_axis=0,
            tiled=True,
        ),
        lax.all_to_all(
            send_gate.reshape(owners, capacity), "expert", split_axis=0, concat_axis=0, tiled=True
        ),
    )
    grads_in = grads_in.reshape(slot_count, out_grad.shape[1])
    acts_in = acts_in.reshape(slot_count, hidden_width)
    gate_rows = gate_in.reshape(slot_count, 1).astype(jnp.float32)
    expert_weight = down_weight[0]
    grad_hidden = lax.dot_general(
        grads_in, expert_weight, (((1,), (1,)), ((), ())), preferred_element_type=jnp.float32
    )
    act_back = (gate_rows * grad_hidden).astype(jnp.bfloat16)
    score_back = jnp.sum(grad_hidden * acts_in.astype(jnp.float32), axis=1).astype(jnp.bfloat16)
    scaled_grad = (gate_rows * grads_in.astype(jnp.float32)).astype(jnp.bfloat16)
    back_rows, back_scores = (
        lax.all_to_all(
            act_back.reshape(owners, capacity, hidden_width),
            "expert",
            split_axis=0,
            concat_axis=0,
            tiled=True,
        ),
        lax.all_to_all(
            score_back.reshape(owners, capacity), "expert", split_axis=0, concat_axis=0, tiled=True
        ),
    )
    weight_term = lax.dot_general(
        acts_in, scaled_grad, (((0,), (0,)), ((), ())), preferred_element_type=jnp.float32
    )
    summed = lax.psum_scatter(
        weight_term.astype(jnp.bfloat16), "dp", scatter_dimension=0, tiled=True
    )
    down_grad = summed[None]
    act_grad = lax.dot_general(
        placement,
        back_rows.reshape(slot_count, hidden_width),
        (((0,), (0,)), ((), ())),
        preferred_element_type=jnp.float32,
    ).astype(jnp.bfloat16)
    score_tok = lax.dot_general(
        placement,
        back_scores.reshape(slot_count, 1),
        (((0,), (0,)), ((), ())),
        preferred_element_type=jnp.float32,
    ).reshape(tok_rows, top_count)
    logit_grad = gate_weights * (
        score_tok - jnp.sum(gate_weights * score_tok, axis=1, keepdims=True)
    )
    return (act_grad.reshape(tok_rows, top_count, hidden_width), logit_grad, down_grad)


def slot_of(y, x, z, c):
    return y * (XS * ZS * CS) + x * (ZS * CS) + z * CS + c


def expert_of(x, z, c):
    return z * (XS * CS) + x * CS + c


def gather_kernel(
    gate_hbm, idx_hbm, acts_hbm, grad_ref, w_hbm,
    act_out, logit_out, down_out,
    gate_ref, idx_ref, acts_ref,
    grads, w_buf, acts_send, acts_in, acts_t, hid, hid_sum, back, total,
    in_sem, own_sem, g_recv, z_send, x_send, y_send, c_send,
    h_send, h_recv, b_send, b_recv,
):
    y = lax.axis_index("dp")
    me = lax.axis_index("expert")
    z = lax.div(me, XS * CS)
    x = lax.rem(lax.div(me, CS), XS)
    c = lax.rem(me, CS)
    n_exp = ZS * XS * CS
    n_dev = 2 * n_exp
    top, tok = idx_ref.shape
    routed, width = acts_ref.shape
    half = width // 2
    model = grad_ref.shape[1]
    lid = y * n_exp + me
    own = slot_of(y, x, z, c)

    def dev(yy, ee):
        return {"dp": yy, "expert": ee}

    barrier = pltpu.get_barrier_semaphore()

    def greet(r, carry):
        other = lax.rem(lid + r, n_dev)
        pl.semaphore_signal(
            barrier, inc=1,
            device_id=dev(lax.div(other, n_exp), lax.rem(other, n_exp)),
            device_id_type=MESH,
        )
        return carry

    lax.fori_loop(1, n_dev, greet, 0)
    part_cols = model // PARTS
    own_grads = [
        pltpu.make_async_copy(
            grad_ref.at[:, pl.ds(p * part_cols, part_cols)], grads.at[p, own], own_sem.at[2 + p]
        )
        for p in range(PARTS)
    ]
    for copy in own_grads:
        copy.start()
    loads = [
        pltpu.make_async_copy(src, dst, in_sem.at[at])
        for at, (src, dst) in enumerate(
            ((gate_hbm, gate_ref), (idx_hbm, idx_ref), (acts_hbm, acts_ref), (w_hbm, w_buf))
        )
    ]
    for load in loads:
        load.start()
    for copy in own_grads:
        copy.wait()
    pl.semaphore_wait(barrier, n_dev - 1)

    def grad_copy(p, slot, sem, yy, ee):
        block = grads.at[p, slot]
        return pltpu.make_async_remote_copy(
            src_ref=block, dst_ref=block, send_sem=sem, recv_sem=g_recv.at[p, slot],
            device_id=dev(yy, ee), device_id_type=MESH,
        )

    def arrived(p, slot):
        grad_copy(p, slot, c_send.at[p, 0], y, expert_of(x, z, 1 - c)).wait_recv()

    sent = []

    def send(copy, when=None):
        if when is None:
            copy.start()
        else:
            pl.when(when)(copy.start)
        sent.append((when, copy))

    def pass_on(p, yy, xx, zz, to_x, to_y, when=None):
        slot = slot_of(yy, xx, zz, c)
        in_plane = xx * ZS + zz
        if to_x:
            at = zz if yy is y else ZS
            send(grad_copy(p, slot, x_send.at[p, at], y, expert_of(1 - x, z, c)), when)
        if to_y:
            send(grad_copy(p, slot, y_send.at[p, in_plane], 1 - y, me), when)
        at = yy * XS * ZS + in_plane
        send(grad_copy(p, slot, c_send.at[p, at], y, expert_of(x, z, 1 - c)), when)

    def along_z(p, zz, way, when):
        slot = slot_of(y, x, zz, c)
        sem = z_send.at[p, (way + 1) // 2, zz]
        send(grad_copy(p, slot, sem, y, expert_of(x, z + way, c)), when)

    for p in range(PARTS):
        for way in (1, -1):
            along_z(p, z, way, (z + way >= 0) & (z + way < ZS))
        pass_on(p, y, x, z, True, True)

    for load in loads[:3]:
        load.wait()
    gate = gate_ref[...]
    gate_half = gate.astype(jnp.bfloat16).astype(jnp.float32)
    idx = idx_ref[...].astype(jnp.float32)
    lane = lax.broadcasted_iota(jnp.int32, (tok, routed), 1)
    line = lax.broadcasted_iota(jnp.int32, (tok, routed), 0)
    widen = (lax.div(lane, top) == line).astype(jnp.float32)
    own_row = lax.broadcasted_iota(jnp.int32, (top, routed), 0) == lax.rem(
        lax.broadcasted_iota(jnp.int32, (top, routed), 1), top
    )
    gate_row = jnp.sum(
        jnp.where(own_row, jnp.dot(gate_half, widen, preferred_element_type=jnp.float32), 0.0),
        axis=0, keepdims=True,
    )
    idx_row = jnp.sum(
        jnp.where(own_row, jnp.dot(idx, widen, preferred_element_type=jnp.float32), 0.0),
        axis=0, keepdims=True,
    )
    rows = n_exp * tok
    row = lax.broadcasted_iota(jnp.int32, (rows, routed), 0)
    col = lax.broadcasted_iota(jnp.int32, (rows, routed), 1)
    row_exp = lax.div(row, tok).astype(jnp.float32)
    place = jnp.where(
        (idx_row == row_exp) & (lax.div(col, top) == lax.rem(row, tok)), gate_row, 0.0
    ).astype(jnp.bfloat16)
    weighted = jnp.dot(place, acts_ref[...], preferred_element_type=jnp.float32)
    weighted = weighted.astype(jnp.bfloat16).reshape(n_exp, tok, width)
    acts_send[0] = weighted[:, :, :half]
    acts_send[1] = weighted[:, :, half:]

    tall_row = lax.broadcasted_iota(jnp.int32, (routed, tok), 0)
    tall_col = lax.broadcasted_iota(jnp.int32, (routed, tok), 1)
    spread = (lax.div(tall_row, top) == tall_col).astype(jnp.float32)
    own_k = (
        lax.broadcasted_iota(jnp.int32, (routed, top), 1)
        == lax.rem(lax.broadcasted_iota(jnp.int32, (routed, top), 0), top)
    ).astype(jnp.float32)

    def column(of):
        wide = lax.dot_general(
            spread, of, (((1,), (1,)), ((), ())), preferred_element_type=jnp.float32
        )
        return jnp.sum(wide * own_k, axis=1, keepdims=True)

    gate_col = column(gate_half)
    idx_col = column(idx)
    row = lax.broadcasted_iota(jnp.int32, (routed, rows), 0)
    col = lax.broadcasted_iota(jnp.int32, (routed, rows), 1)
    pick = (
        (idx_col == lax.div(col, tok).astype(jnp.float32))
        & (lax.div(row, top) == lax.rem(col, tok))
    ).astype(jnp.float32).astype(jnp.bfloat16)

    def receive(p, yy, xx, dist, to_z, to_x, to_y):
        for way in (1, -1) if dist else (1,):
            zz = z - way * dist
            there = (zz >= 0) & (zz < ZS) if dist else None
            slot = slot_of(yy, xx, zz, c)
            if dist:
                pl.when(there)(functools.partial(arrived, p, slot))
            else:
                arrived(p, slot)
            if to_z:
                along_z(p, zz, way, there & (z + way >= 0) & (z + way < ZS))
            pass_on(p, yy, xx, zz, to_x, to_y, there)

    def from_z(p, dist):
        receive(p, y, x, dist, True, True, True)

    def from_x(p, dist):
        receive(p, y, 1 - x, dist, False, False, dist != 2)

    def from_group(p, xx, dist):
        receive(p, 1 - y, xx, dist, False, xx is x and dist == 2, False)

    def acts_copy(r):
        other = lax.rem(lid + r, n_dev)
        yy, ee = lax.div(other, n_exp), lax.rem(other, n_exp)
        return pltpu.make_async_remote_copy(
            src_ref=acts_send.at[yy, ee], dst_ref=acts_in.at[own],
            send_sem=h_send.at[r], recv_sem=h_recv.at[own],
            device_id=dev(yy, ee), device_id_type=MESH,
        )

    def acts_start(r, carry):
        acts_copy(r).start()
        return carry

    own_acts = pltpu.make_async_copy(acts_send.at[y, me], acts_in.at[own], own_sem.at[1])

    def back_copy(slot, zz, xx, cc):
        return pltpu.make_async_remote_copy(
            src_ref=hid.at[slot], dst_ref=back.at[me],
            send_sem=b_send.at[slot], recv_sem=b_recv.at[me],
            device_id=dev(y, expert_of(xx, zz, cc)), device_id_type=MESH,
        )

    per_x = ZS * CS
    tile = model // 4

    def hidden(p):
        part = lax.dot_general(
            grads[p, pl.ds(y * n_exp, n_exp)].reshape(n_exp * tok, part_cols),
            w_buf[:, pl.ds(p * part_cols, part_cols)],
            (((1,), (1,)), ((), ())), preferred_element_type=jnp.float32,
        )
        if p:
            part = part + hid_sum[...]
        if p < PARTS - 1:
            hid_sum[...] = part
        else:
            hid[...] = part.astype(jnp.bfloat16).reshape(n_exp, tok, width)

    def mates(p, group):
        for xx in (x, 1 - x):
            for zz in range(ZS):
                arrived(p, slot_of(group, xx, zz, 1 - c))

    parts = range(PARTS)
    for p in parts:
        from_z(p, 1)
    for p in parts:
        from_x(p, 0)
    for p in parts:
        from_z(p, 2)
    for p in parts:
        from_x(p, 1)
    for p in parts:
        from_z(p, 3)
    lax.fori_loop(1, n_dev, acts_start, 0)
    own_acts.start()
    for p in parts:
        from_x(p, 2)
    for dist in range(2):
        for p in parts:
            from_group(p, x, dist)
    loads[3].wait()
    for p in parts:
        from_x(p, 3)
        mates(p, y)
        hidden(p)
    own_back = pltpu.make_async_copy(hid.at[own - y * n_exp], back.at[me], own_sem.at[0])
    own_back.start()

    def each_back():
        for xx in (1 - x, x):
            for r in range(per_x):
                at = lax.rem(z * CS + c + r, per_x)
                if xx is not x or r:
                    yield back_copy(xx * per_x + at, lax.div(at, CS), xx, lax.rem(at, CS))

    for copy in each_back():
        copy.start()

    def acts_wait(r, group):
        ee = lax.rem(me + r, n_exp)
        slot = slot_of(
            group, lax.rem(lax.div(ee, CS), XS), lax.div(ee, XS * CS), lax.rem(ee, CS)
        )
        pltpu.make_async_remote_copy(
            src_ref=acts_send.at[0, 0], dst_ref=acts_in.at[slot],
            send_sem=h_send.at[0], recv_sem=h_recv.at[slot],
            device_id=dev(1 - y, me), device_id_type=MESH,
        ).wait_recv()
        return group

    def turn(group, at):
        rows_in = acts_in[pl.ds(group * n_exp, n_exp)].reshape(n_exp * tok, half)
        acts_t[at] = rows_in.T

    def down_part(group, at, n):
        p = lax.div(n * tile, part_cols)
        cols = pl.ds(pl.multiple_of(lax.rem(n * tile, part_cols), tile), tile)
        return jnp.dot(
            acts_t[at], grads[p, pl.ds(group * n_exp, n_exp), :, cols].reshape(n_exp * tok, tile),
            preferred_element_type=jnp.float32,
        )

    for dist in range(2, ZS):
        for p in parts:
            from_group(p, x, dist)

    lax.fori_loop(1, n_exp, acts_wait, y)
    own_acts.wait()
    turn(y, 0)

    @pl.loop(0, model // tile)
    def _(n):
        cols = pl.ds(pl.multiple_of(n * tile, tile), tile)
        total[:, cols] = down_part(y, 0, n)

    for dist in range(ZS):
        for p in parts:
            from_group(p, 1 - x, dist)

    lax.fori_loop(0, n_exp, acts_wait, 1 - y)
    turn(1 - y, 1)
    for p in parts:
        mates(p, 1 - y)

    @pl.loop(0, model // tile)
    def _(n):
        cols = pl.ds(pl.multiple_of(n * tile, tile), tile)
        down_out[:, cols] = (total[:, cols] + down_part(1 - y, 1, n)).astype(jnp.bfloat16)

    def back_wait(r, carry):
        ee = lax.rem(me + r, n_exp)
        pltpu.make_async_remote_copy(
            src_ref=hid.at[0], dst_ref=back.at[ee],
            send_sem=b_send.at[0], recv_sem=b_recv.at[ee],
            device_id=dev(1 - y, me), device_id_type=MESH,
        ).wait_recv()
        return carry

    lax.fori_loop(1, n_exp, back_wait, 0)
    own_back.wait()
    picked = jnp.dot(pick, back[...].reshape(rows, width), preferred_element_type=jnp.float32)
    act_out[...] = (gate_col * picked).astype(jnp.bfloat16)
    score = jnp.sum(picked * acts_ref[...].astype(jnp.float32), axis=1, keepdims=True)
    score = score.astype(jnp.bfloat16).astype(jnp.float32)
    score = jnp.dot(own_row.astype(jnp.float32), score * spread, preferred_element_type=jnp.float32)
    logit_out[...] = gate * (score - jnp.sum(gate * score, axis=0, keepdims=True))

    for when, copy in sent:
        if when is None:
            copy.wait_send()
        else:
            pl.when(when)(copy.wait_send)

    def acts_sent(r, carry):
        acts_copy(r).wait_send()
        return carry

    lax.fori_loop(1, n_dev, acts_sent, 0)
    for copy in each_back():
        copy.wait_send()


def gathered_shards(out_grad, hidden_acts, gate_weights, expert_idx, down_weight):
    tok, top = expert_idx.shape
    model = out_grad.shape[1]
    width = hidden_acts.shape[2]
    half = width // 2
    n_exp = ZS * XS * CS
    n_dev = 2 * n_exp
    dma = pltpu.SemaphoreType.DMA
    vmem = pl.BlockSpec(memory_space=pltpu.VMEM)
    hbm = pl.BlockSpec(memory_space=pltpu.HBM)
    act, logit, down = pl.pallas_call(
        gather_kernel,
        out_shape=(
            jax.ShapeDtypeStruct((tok * top, width), jnp.bfloat16),
            jax.ShapeDtypeStruct((top, tok), jnp.float32),
            jax.ShapeDtypeStruct((half, model), jnp.bfloat16),
        ),
        in_specs=[hbm] * 5,
        out_specs=(vmem, vmem, vmem),
        scratch_shapes=[
            pltpu.VMEM((top, tok), jnp.float32),
            pltpu.VMEM((top, tok), jnp.int32),
            pltpu.VMEM((tok * top, width), jnp.bfloat16),
            pltpu.VMEM((PARTS, n_dev, tok, model // PARTS), jnp.bfloat16),
            pltpu.VMEM((width, model), jnp.bfloat16),
            pltpu.VMEM((2, n_exp, tok, half), jnp.bfloat16),
            pltpu.VMEM((n_dev, tok, half), jnp.bfloat16),
            pltpu.VMEM((2, half, n_exp * tok), jnp.bfloat16),
            pltpu.VMEM((n_exp, tok, width), jnp.bfloat16),
            pltpu.VMEM((n_exp * tok, width), jnp.float32),
            pltpu.VMEM((n_exp, tok, width), jnp.bfloat16),
            pltpu.VMEM((half, model), jnp.float32),
            dma((4,)),
            dma((2 + PARTS,)),
            dma((PARTS, n_dev)),
            dma((PARTS, 2, ZS)),
            dma((PARTS, ZS + 1)),
            dma((PARTS, XS * ZS)),
            dma((PARTS, 2 * XS * ZS)),
            dma((n_dev,)),
            dma((n_dev,)),
            dma((n_exp,)),
            dma((n_exp,)),
        ],
        compiler_params=pltpu.CompilerParams(
            collective_id=0, has_side_effects=True, vmem_limit_bytes=36 * 1024 * 1024
        ),
        cost_estimate=pl.CostEstimate(
            flops=6 * n_exp * tok * model * width, bytes_accessed=3 * width * model * 2,
            transcendentals=0,
        ),
    )(
        *(
            pltpu.with_memory_space_constraint(array, pltpu.HBM)
            for array in (
                gate_weights.T, expert_idx.T, hidden_acts.reshape(tok * top, width), out_grad,
                down_weight.reshape(width, model),
            )
        )
    )
    return act.reshape(tok, top, width), logit.T, down[None]


def solution(mesh):
    gathered = mesh.shape["dp"] == 2 and mesh.shape["expert"] == ZS * XS * CS
    return jax.shard_map(
        gathered_shards if gathered else routed_shards,
        mesh=mesh,
        in_specs=(
            P(("dp", "expert"), None),
            P(("dp", "expert"), None, None),
            P(("dp", "expert"), None),
            P(("dp", "expert"), None),
            P("expert", None, None),
        ),
        out_specs=(
            P(("dp", "expert"), None, None),
            P(("dp", "expert"), None),
            P("expert", "dp", None),
        ),
        check_vma=False,
    )
```

```python
import functools

import jax
import jax.numpy as jnp
from jax import lax
from jax.experimental import pallas as pl
from jax.experimental.pallas import tpu as pltpu
from jax.sharding import PartitionSpec as P

MESH = pl.DeviceIdType.MESH
ZS, XS, CS = 4, 2, 2
STRIPS = 4
PARTS = 2


def routed_shards(out_grad, hidden_acts, gate_weights, expert_idx, down_weight):
    tok_rows, top_count = expert_idx.shape
    routed = tok_rows * top_count
    hidden_width = hidden_acts.shape[2]
    owners = lax.axis_size("expert")
    experts = owners * down_weight.shape[0]
    capacity = min(tok_rows, max(2, (3 * tok_rows * top_count + 2 * experts - 1) // (2 * experts)))
    slot_count = experts * capacity
    flat_expert = expert_idx.reshape(routed)
    member = (flat_expert[:, None] == jnp.arange(experts, dtype=jnp.int32)[None, :]).astype(
        jnp.bfloat16
    )
    row_line = jnp.arange(routed, dtype=jnp.int32)
    earlier_mask = (row_line[:, None] > row_line[None, :]).astype(jnp.bfloat16)
    earlier = jnp.dot(earlier_mask, member, preferred_element_type=jnp.float32)
    position = jnp.sum(earlier * member.astype(jnp.float32), axis=1).astype(jnp.int32)
    slot_index = flat_expert * capacity + position
    placement = (jnp.arange(slot_count, dtype=jnp.int32)[:, None] == slot_index[None, :]).astype(
        jnp.bfloat16
    )
    token_place = jnp.sum(placement.reshape(slot_count, tok_rows, top_count), axis=2)
    gate_half = lax.optimization_barrier(gate_weights.astype(jnp.bfloat16))
    send_grads = jnp.dot(token_place, out_grad, preferred_element_type=jnp.float32).astype(
        jnp.bfloat16
    )
    send_acts = jnp.dot(
        placement, hidden_acts.reshape(routed, hidden_width), preferred_element_type=jnp.float32
    ).astype(jnp.bfloat16)
    send_gate = jnp.dot(
        placement, gate_half.reshape(routed, 1), preferred_element_type=jnp.float32
    ).astype(jnp.bfloat16)
    grads_in, acts_in, gate_in = (
        lax.all_to_all(
            send_grads.reshape(owners, capacity, out_grad.shape[1]),
            "expert",
            split_axis=0,
            concat_axis=0,
            tiled=True,
        ),
        lax.all_to_all(
            send_acts.reshape(owners, capacity, hidden_width),
            "expert",
            split_axis=0,
            concat_axis=0,
            tiled=True,
        ),
        lax.all_to_all(
            send_gate.reshape(owners, capacity), "expert", split_axis=0, concat_axis=0, tiled=True
        ),
    )
    grads_in = grads_in.reshape(slot_count, out_grad.shape[1])
    acts_in = acts_in.reshape(slot_count, hidden_width)
    gate_rows = gate_in.reshape(slot_count, 1).astype(jnp.float32)
    expert_weight = down_weight[0]
    grad_hidden = lax.dot_general(
        grads_in, expert_weight, (((1,), (1,)), ((), ())), preferred_element_type=jnp.float32
    )
    act_back = (gate_rows * grad_hidden).astype(jnp.bfloat16)
    score_back = jnp.sum(grad_hidden * acts_in.astype(jnp.float32), axis=1).astype(jnp.bfloat16)
    scaled_grad = (gate_rows * grads_in.astype(jnp.float32)).astype(jnp.bfloat16)
    back_rows, back_scores = (
        lax.all_to_all(
            act_back.reshape(owners, capacity, hidden_width),
            "expert",
            split_axis=0,
            concat_axis=0,
            tiled=True,
        ),
        lax.all_to_all(
            score_back.reshape(owners, capacity), "expert", split_axis=0, concat_axis=0, tiled=True
        ),
    )
    weight_term = lax.dot_general(
        acts_in, scaled_grad, (((0,), (0,)), ((), ())), preferred_element_type=jnp.float32
    )
    summed = lax.psum_scatter(
        weight_term.astype(jnp.bfloat16), "dp", scatter_dimension=0, tiled=True
    )
    down_grad = summed[None]
    act_grad = lax.dot_general(
        placement,
        back_rows.reshape(slot_count, hidden_width),
        (((0,), (0,)), ((), ())),
        preferred_element_type=jnp.float32,
    ).astype(jnp.bfloat16)
    score_tok = lax.dot_general(
        placement,
        back_scores.reshape(slot_count, 1),
        (((0,), (0,)), ((), ())),
        preferred_element_type=jnp.float32,
    ).reshape(tok_rows, top_count)
    logit_grad = gate_weights * (
        score_tok - jnp.sum(gate_weights * score_tok, axis=1, keepdims=True)
    )
    return (act_grad.reshape(tok_rows, top_count, hidden_width), logit_grad, down_grad)


def slot_of(y, x, z, c):
    return y * (XS * ZS * CS) + x * (ZS * CS) + z * CS + c


def expert_of(x, z, c):
    return z * (XS * CS) + x * CS + c


def gather_kernel(
    gate_hbm, idx_hbm, acts_hbm, grad_ref, w_hbm,
    act_out, logit_out, down_out,
    gate_ref, idx_ref, acts_ref,
    grads, w_buf, acts_send, acts_in, acts_t, hid, hid_sum, back, total,
    in_sem, own_sem, g_recv, z_send, x_send, y_send, c_send,
    h_send, h_recv, b_send, b_recv,
):
    y = lax.axis_index("dp")
    me = lax.axis_index("expert")
    z = lax.div(me, XS * CS)
    x = lax.rem(lax.div(me, CS), XS)
    c = lax.rem(me, CS)
    n_exp = ZS * XS * CS
    n_dev = 2 * n_exp
    top, tok = idx_ref.shape
    routed, width = acts_ref.shape
    half = width // 2
    model = grad_ref.shape[1]
    lid = y * n_exp + me
    own = slot_of(y, x, z, c)

    def dev(yy, ee):
        return {"dp": yy, "expert": ee}

    part_cols = model // PARTS
    own_grads = [
        pltpu.make_async_copy(
            grad_ref.at[:, pl.ds(p * part_cols, part_cols)], grads.at[p, own], own_sem.at[2 + p]
        )
        for p in range(PARTS)
    ]
    for copy in own_grads:
        copy.start()

    barrier = pltpu.get_barrier_semaphore()

    def greet(r, carry):
        other = lax.rem(lid + r, n_dev)
        pl.semaphore_signal(
            barrier, inc=1,
            device_id=dev(lax.div(other, n_exp), lax.rem(other, n_exp)),
            device_id_type=MESH,
        )
        return carry

    lax.fori_loop(1, n_dev, greet, 0)
    loads = [
        pltpu.make_async_copy(src, dst, in_sem.at[at])
        for at, (src, dst) in enumerate(
            ((gate_hbm, gate_ref), (idx_hbm, idx_ref), (acts_hbm, acts_ref), (w_hbm, w_buf))
        )
    ]
    for load in loads:
        load.start()
    for copy in own_grads:
        copy.wait()
    pl.semaphore_wait(barrier, n_dev - 1)

    def grad_copy(p, slot, sem, yy, ee):
        block = grads.at[p, slot]
        return pltpu.make_async_remote_copy(
            src_ref=block, dst_ref=block, send_sem=sem, recv_sem=g_recv.at[p, slot],
            device_id=dev(yy, ee), device_id_type=MESH,
        )

    def arrived(p, slot):
        grad_copy(p, slot, c_send.at[p, 0], y, expert_of(x, z, 1 - c)).wait_recv()

    sent = []

    def send(copy, when=None):
        if when is None:
            copy.start()
        else:
            pl.when(when)(copy.start)
        sent.append((when, copy))

    def pass_on(p, yy, xx, zz, to_x, to_y, when=None):
        slot = slot_of(yy, xx, zz, c)
        in_plane = xx * ZS + zz
        if to_x:
            at = zz if yy is y else ZS
            send(grad_copy(p, slot, x_send.at[p, at], y, expert_of(1 - x, z, c)), when)
        if to_y:
            send(grad_copy(p, slot, y_send.at[p, in_plane], 1 - y, me), when)
        at = yy * XS * ZS + in_plane
        send(grad_copy(p, slot, c_send.at[p, at], y, expert_of(x, z, 1 - c)), when)

    def along_z(p, zz, way, when):
        slot = slot_of(y, x, zz, c)
        sem = z_send.at[p, (way + 1) // 2, zz]
        send(grad_copy(p, slot, sem, y, expert_of(x, z + way, c)), when)

    for p in range(PARTS):
        for way in (1, -1):
            along_z(p, z, way, (z + way >= 0) & (z + way < ZS))
        pass_on(p, y, x, z, True, True)

    for load in loads[:3]:
        load.wait()
    gate = gate_ref[...]
    gate_half = gate.astype(jnp.bfloat16).astype(jnp.float32)
    idx = idx_ref[...].astype(jnp.float32)
    lane = lax.broadcasted_iota(jnp.int32, (tok, routed), 1)
    line = lax.broadcasted_iota(jnp.int32, (tok, routed), 0)
    widen = (lax.div(lane, top) == line).astype(jnp.float32)
    own_row = lax.broadcasted_iota(jnp.int32, (top, routed), 0) == lax.rem(
        lax.broadcasted_iota(jnp.int32, (top, routed), 1), top
    )
    gate_row = jnp.sum(
        jnp.where(own_row, jnp.dot(gate_half, widen, preferred_element_type=jnp.float32), 0.0),
        axis=0, keepdims=True,
    )
    idx_row = jnp.sum(
        jnp.where(own_row, jnp.dot(idx, widen, preferred_element_type=jnp.float32), 0.0),
        axis=0, keepdims=True,
    )
    rows = n_exp * tok
    row = lax.broadcasted_iota(jnp.int32, (rows, routed), 0)
    col = lax.broadcasted_iota(jnp.int32, (rows, routed), 1)
    row_exp = lax.div(row, tok).astype(jnp.float32)
    place = jnp.where(
        (idx_row == row_exp) & (lax.div(col, top) == lax.rem(row, tok)), gate_row, 0.0
    ).astype(jnp.bfloat16)
    weighted = jnp.dot(place, acts_ref[...], preferred_element_type=jnp.float32)
    weighted = weighted.astype(jnp.bfloat16).reshape(n_exp, tok, width)
    acts_send[0] = weighted[:, :, :half]
    acts_send[1] = weighted[:, :, half:]

    tall_row = lax.broadcasted_iota(jnp.int32, (routed, tok), 0)
    tall_col = lax.broadcasted_iota(jnp.int32, (routed, tok), 1)
    spread = (lax.div(tall_row, top) == tall_col).astype(jnp.float32)
    own_k = (
        lax.broadcasted_iota(jnp.int32, (routed, top), 1)
        == lax.rem(lax.broadcasted_iota(jnp.int32, (routed, top), 0), top)
    ).astype(jnp.float32)

    def column(of):
        wide = lax.dot_general(
            spread, of, (((1,), (1,)), ((), ())), preferred_element_type=jnp.float32
        )
        return jnp.sum(wide * own_k, axis=1, keepdims=True)

    gate_col = column(gate_half)
    idx_col = column(idx)
    row = lax.broadcasted_iota(jnp.int32, (routed, rows), 0)
    col = lax.broadcasted_iota(jnp.int32, (routed, rows), 1)
    pick = (
        (idx_col == lax.div(col, tok).astype(jnp.float32))
        & (lax.div(row, top) == lax.rem(col, tok))
    ).astype(jnp.float32).astype(jnp.bfloat16)

    def receive(p, yy, xx, dist, to_z, to_x, to_y):
        for way in (1, -1) if dist else (1,):
            zz = z - way * dist
            there = (zz >= 0) & (zz < ZS) if dist else None
            slot = slot_of(yy, xx, zz, c)
            if dist:
                pl.when(there)(functools.partial(arrived, p, slot))
            else:
                arrived(p, slot)
            if to_z:
                along_z(p, zz, way, there & (z + way >= 0) & (z + way < ZS))
            pass_on(p, yy, xx, zz, to_x, to_y, there)

    def from_z(p, dist):
        receive(p, y, x, dist, True, True, True)

    def from_x(p, dist):
        receive(p, y, 1 - x, dist, False, False, dist != 2)

    def from_group(p, xx, dist):
        receive(p, 1 - y, xx, dist, False, xx is x and dist == 2, False)

    def acts_copy(r):
        other = lax.rem(lid + r, n_dev)
        yy, ee = lax.div(other, n_exp), lax.rem(other, n_exp)
        return pltpu.make_async_remote_copy(
            src_ref=acts_send.at[yy, ee], dst_ref=acts_in.at[own],
            send_sem=h_send.at[r], recv_sem=h_recv.at[own],
            device_id=dev(yy, ee), device_id_type=MESH,
        )

    def acts_start(r, carry):
        acts_copy(r).start()
        return carry

    own_acts = pltpu.make_async_copy(acts_send.at[y, me], acts_in.at[own], own_sem.at[1])

    def back_copy(slot, zz, xx, cc):
        return pltpu.make_async_remote_copy(
            src_ref=hid.at[slot], dst_ref=back.at[me],
            send_sem=b_send.at[slot], recv_sem=b_recv.at[me],
            device_id=dev(y, expert_of(xx, zz, cc)), device_id_type=MESH,
        )

    per_x = ZS * CS
    tile = model // 4

    def hidden(p):
        part = lax.dot_general(
            grads[p, pl.ds(y * n_exp, n_exp)].reshape(n_exp * tok, part_cols),
            w_buf[:, pl.ds(p * part_cols, part_cols)],
            (((1,), (1,)), ((), ())), preferred_element_type=jnp.float32,
        )
        if p:
            part = part + hid_sum[...]
        if p < PARTS - 1:
            hid_sum[...] = part
        else:
            hid[...] = part.astype(jnp.bfloat16).reshape(n_exp, tok, width)

    def mates(p, group):
        for xx in (x, 1 - x):
            for zz in range(ZS):
                arrived(p, slot_of(group, xx, zz, 1 - c))

    parts = range(PARTS)
    for p in parts:
        from_z(p, 1)
    for p in parts:
        from_x(p, 0)
    for p in parts:
        from_z(p, 2)
    for p in parts:
        from_x(p, 1)
    for p in parts:
        from_z(p, 3)
    for p in parts:
        from_x(p, 2)
    lax.fori_loop(1, n_dev, acts_start, 0)
    own_acts.start()
    for dist in range(2):
        for p in parts:
            from_group(p, x, dist)
    loads[3].wait()
    for p in parts:
        from_x(p, 3)
        mates(p, y)
        hidden(p)
    own_back = pltpu.make_async_copy(hid.at[own - y * n_exp], back.at[me], own_sem.at[0])
    own_back.start()

    def each_back():
        for xx in (1 - x, x):
            for r in range(per_x):
                at = lax.rem(z * CS + c + r, per_x)
                if xx is not x or r:
                    yield back_copy(xx * per_x + at, lax.div(at, CS), xx, lax.rem(at, CS))

    for copy in each_back():
        copy.start()

    def acts_wait(r, group):
        ee = lax.rem(me + r, n_exp)
        slot = slot_of(
            group, lax.rem(lax.div(ee, CS), XS), lax.div(ee, XS * CS), lax.rem(ee, CS)
        )
        pltpu.make_async_remote_copy(
            src_ref=acts_send.at[0, 0], dst_ref=acts_in.at[slot],
            send_sem=h_send.at[0], recv_sem=h_recv.at[slot],
            device_id=dev(1 - y, me), device_id_type=MESH,
        ).wait_recv()
        return group

    def turn(group, at):
        rows_in = acts_in[pl.ds(group * n_exp, n_exp)].reshape(n_exp * tok, half)
        acts_t[at] = rows_in.T

    def down_part(group, at, n):
        p = lax.div(n * tile, part_cols)
        cols = pl.ds(pl.multiple_of(lax.rem(n * tile, part_cols), tile), tile)
        return jnp.dot(
            acts_t[at], grads[p, pl.ds(group * n_exp, n_exp), :, cols].reshape(n_exp * tok, tile),
            preferred_element_type=jnp.float32,
        )

    for dist in range(2, ZS):
        for p in parts:
            from_group(p, x, dist)

    for dist in range(ZS):
        for p in parts:
            from_group(p, 1 - x, dist)

    lax.fori_loop(1, n_exp, acts_wait, y)
    own_acts.wait()
    turn(y, 0)

    @pl.loop(0, model // tile)
    def _(n):
        cols = pl.ds(pl.multiple_of(n * tile, tile), tile)
        total[:, cols] = down_part(y, 0, n)

    lax.fori_loop(0, n_exp, acts_wait, 1 - y)
    turn(1 - y, 1)
    for p in parts:
        mates(p, 1 - y)

    @pl.loop(0, model // tile)
    def _(n):
        cols = pl.ds(pl.multiple_of(n * tile, tile), tile)
        down_out[:, cols] = (total[:, cols] + down_part(1 - y, 1, n)).astype(jnp.bfloat16)

    for when, copy in sent:
        if when is None:
            copy.wait_send()
        else:
            pl.when(when)(copy.wait_send)

    def acts_sent(r, carry):
        acts_copy(r).wait_send()
        return carry

    lax.fori_loop(1, n_dev, acts_sent, 0)
    for copy in each_back():
        copy.wait_send()

    def back_wait(r, carry):
        ee = lax.rem(me + r, n_exp)
        pltpu.make_async_remote_copy(
            src_ref=hid.at[0], dst_ref=back.at[ee],
            send_sem=b_send.at[0], recv_sem=b_recv.at[ee],
            device_id=dev(1 - y, me), device_id_type=MESH,
        ).wait_recv()
        return carry

    lax.fori_loop(1, n_exp, back_wait, 0)
    own_back.wait()
    picked = jnp.dot(pick, back[...].reshape(rows, width), preferred_element_type=jnp.float32)
    act_out[...] = (gate_col * picked).astype(jnp.bfloat16)
    score = jnp.sum(picked * acts_ref[...].astype(jnp.float32), axis=1, keepdims=True)
    score = score.astype(jnp.bfloat16).astype(jnp.float32)
    score = jnp.dot(own_row.astype(jnp.float32), score * spread, preferred_element_type=jnp.float32)
    logit_out[...] = gate * (score - jnp.sum(gate * score, axis=0, keepdims=True))


def store_kernel(*refs):
    results, outs, sems = refs[:3], refs[3:6], refs[6]
    copies = []
    for src, dst in zip(results, outs):
        rows = src.shape[0]
        step = rows // STRIPS if rows % (16 * STRIPS) == 0 else rows
        for at in range(0, rows, step):
            strip = pl.ds(at, step)
            copies.append(
                pltpu.make_async_copy(src.at[strip], dst.at[strip], sems.at[len(copies)])
            )
    for copy in copies[::-1]:
        copy.start()
    for copy in copies:
        copy.wait()


def gathered_shards(out_grad, hidden_acts, gate_weights, expert_idx, down_weight):
    tok, top = expert_idx.shape
    model = out_grad.shape[1]
    width = hidden_acts.shape[2]
    half = width // 2
    n_exp = ZS * XS * CS
    n_dev = 2 * n_exp
    dma = pltpu.SemaphoreType.DMA
    vmem = pl.BlockSpec(memory_space=pltpu.VMEM)
    hbm = pl.BlockSpec(memory_space=pltpu.HBM)
    act, logit, down = pl.pallas_call(
        gather_kernel,
        out_shape=(
            jax.ShapeDtypeStruct((tok * top, width), jnp.bfloat16),
            jax.ShapeDtypeStruct((top, tok), jnp.float32),
            jax.ShapeDtypeStruct((half, model), jnp.bfloat16),
        ),
        in_specs=[hbm] * 5,
        out_specs=(vmem, vmem, vmem),
        scratch_shapes=[
            pltpu.VMEM((top, tok), jnp.float32),
            pltpu.VMEM((top, tok), jnp.int32),
            pltpu.VMEM((tok * top, width), jnp.bfloat16),
            pltpu.VMEM((PARTS, n_dev, tok, model // PARTS), jnp.bfloat16),
            pltpu.VMEM((width, model), jnp.bfloat16),
            pltpu.VMEM((2, n_exp, tok, half), jnp.bfloat16),
            pltpu.VMEM((n_dev, tok, half), jnp.bfloat16),
            pltpu.VMEM((2, half, n_exp * tok), jnp.bfloat16),
            pltpu.VMEM((n_exp, tok, width), jnp.bfloat16),
            pltpu.VMEM((n_exp * tok, width), jnp.float32),
            pltpu.VMEM((n_exp, tok, width), jnp.bfloat16),
            pltpu.VMEM((half, model), jnp.float32),
            dma((4,)),
            dma((2 + PARTS,)),
            dma((PARTS, n_dev)),
            dma((PARTS, 2, ZS)),
            dma((PARTS, ZS + 1)),
            dma((PARTS, XS * ZS)),
            dma((PARTS, 2 * XS * ZS)),
            dma((n_dev,)),
            dma((n_dev,)),
            dma((n_exp,)),
            dma((n_exp,)),
        ],
        compiler_params=pltpu.CompilerParams(
            collective_id=0, has_side_effects=True, vmem_limit_bytes=36 * 1024 * 1024
        ),
        cost_estimate=pl.CostEstimate(
            flops=6 * n_exp * tok * model * width, bytes_accessed=3 * width * model * 2,
            transcendentals=0,
        ),
    )(
        *(
            pltpu.with_memory_space_constraint(array, pltpu.HBM)
            for array in (
                gate_weights.T, expert_idx.T, hidden_acts.reshape(tok * top, width), out_grad,
                down_weight.reshape(width, model),
            )
        )
    )
    results = (act, logit, down)
    act, logit, down = pl.pallas_call(
        store_kernel,
        out_shape=tuple(jax.ShapeDtypeStruct(of.shape, of.dtype) for of in results),
        in_specs=[vmem] * 3,
        out_specs=(hbm,) * 3,
        scratch_shapes=[dma((3 * STRIPS,))],
        compiler_params=pltpu.CompilerParams(vmem_limit_bytes=16 * 1024 * 1024),
    )(*results)
    return act.reshape(tok, top, width), logit.T, down[None]


def solution(mesh):
    gathered = mesh.shape["dp"] == 2 and mesh.shape["expert"] == ZS * XS * CS
    return jax.shard_map(
        gathered_shards if gathered else routed_shards,
        mesh=mesh,
        in_specs=(
            P(("dp", "expert"), None),
            P(("dp", "expert"), None, None),
            P(("dp", "expert"), None),
            P(("dp", "expert"), None),
            P("expert", None, None),
        ),
        out_specs=(
            P(("dp", "expert"), None, None),
            P(("dp", "expert"), None),
            P("expert", "dp", None),
        ),
        check_vma=False,
    )
```

```python
import functools

import jax
import jax.numpy as jnp
from jax import lax
from jax.experimental import pallas as pl
from jax.experimental.pallas import tpu as pltpu
from jax.sharding import PartitionSpec as P

MESH = pl.DeviceIdType.MESH
ZS, XS, CS = 4, 2, 2
STRIPS = 4
PARTS = 2


def routed_shards(out_grad, hidden_acts, gate_weights, expert_idx, down_weight):
    tok_rows, top_count = expert_idx.shape
    routed = tok_rows * top_count
    hidden_width = hidden_acts.shape[2]
    owners = lax.axis_size("expert")
    experts = owners * down_weight.shape[0]
    capacity = min(tok_rows, max(2, (3 * tok_rows * top_count + 2 * experts - 1) // (2 * experts)))
    slot_count = experts * capacity
    flat_expert = expert_idx.reshape(routed)
    member = (flat_expert[:, None] == jnp.arange(experts, dtype=jnp.int32)[None, :]).astype(
        jnp.bfloat16
    )
    row_line = jnp.arange(routed, dtype=jnp.int32)
    earlier_mask = (row_line[:, None] > row_line[None, :]).astype(jnp.bfloat16)
    earlier = jnp.dot(earlier_mask, member, preferred_element_type=jnp.float32)
    position = jnp.sum(earlier * member.astype(jnp.float32), axis=1).astype(jnp.int32)
    slot_index = flat_expert * capacity + position
    placement = (jnp.arange(slot_count, dtype=jnp.int32)[:, None] == slot_index[None, :]).astype(
        jnp.bfloat16
    )
    token_place = jnp.sum(placement.reshape(slot_count, tok_rows, top_count), axis=2)
    gate_half = lax.optimization_barrier(gate_weights.astype(jnp.bfloat16))
    send_grads = jnp.dot(token_place, out_grad, preferred_element_type=jnp.float32).astype(
        jnp.bfloat16
    )
    send_acts = jnp.dot(
        placement, hidden_acts.reshape(routed, hidden_width), preferred_element_type=jnp.float32
    ).astype(jnp.bfloat16)
    send_gate = jnp.dot(
        placement, gate_half.reshape(routed, 1), preferred_element_type=jnp.float32
    ).astype(jnp.bfloat16)
    grads_in, acts_in, gate_in = (
        lax.all_to_all(
            send_grads.reshape(owners, capacity, out_grad.shape[1]),
            "expert",
            split_axis=0,
            concat_axis=0,
            tiled=True,
        ),
        lax.all_to_all(
            send_acts.reshape(owners, capacity, hidden_width),
            "expert",
            split_axis=0,
            concat_axis=0,
            tiled=True,
        ),
        lax.all_to_all(
            send_gate.reshape(owners, capacity), "expert", split_axis=0, concat_axis=0, tiled=True
        ),
    )
    grads_in = grads_in.reshape(slot_count, out_grad.shape[1])
    acts_in = acts_in.reshape(slot_count, hidden_width)
    gate_rows = gate_in.reshape(slot_count, 1).astype(jnp.float32)
    expert_weight = down_weight[0]
    grad_hidden = lax.dot_general(
        grads_in, expert_weight, (((1,), (1,)), ((), ())), preferred_element_type=jnp.float32
    )
    act_back = (gate_rows * grad_hidden).astype(jnp.bfloat16)
    score_back = jnp.sum(grad_hidden * acts_in.astype(jnp.float32), axis=1).astype(jnp.bfloat16)
    scaled_grad = (gate_rows * grads_in.astype(jnp.float32)).astype(jnp.bfloat16)
    back_rows, back_scores = (
        lax.all_to_all(
            act_back.reshape(owners, capacity, hidden_width),
            "expert",
            split_axis=0,
            concat_axis=0,
            tiled=True,
        ),
        lax.all_to_all(
            score_back.reshape(owners, capacity), "expert", split_axis=0, concat_axis=0, tiled=True
        ),
    )
    weight_term = lax.dot_general(
        acts_in, scaled_grad, (((0,), (0,)), ((), ())), preferred_element_type=jnp.float32
    )
    summed = lax.psum_scatter(
        weight_term.astype(jnp.bfloat16), "dp", scatter_dimension=0, tiled=True
    )
    down_grad = summed[None]
    act_grad = lax.dot_general(
        placement,
        back_rows.reshape(slot_count, hidden_width),
        (((0,), (0,)), ((), ())),
        preferred_element_type=jnp.float32,
    ).astype(jnp.bfloat16)
    score_tok = lax.dot_general(
        placement,
        back_scores.reshape(slot_count, 1),
        (((0,), (0,)), ((), ())),
        preferred_element_type=jnp.float32,
    ).reshape(tok_rows, top_count)
    logit_grad = gate_weights * (
        score_tok - jnp.sum(gate_weights * score_tok, axis=1, keepdims=True)
    )
    return (act_grad.reshape(tok_rows, top_count, hidden_width), logit_grad, down_grad)


def slot_of(y, x, z, c):
    return y * (XS * ZS * CS) + x * (ZS * CS) + z * CS + c


def expert_of(x, z, c):
    return z * (XS * CS) + x * CS + c


def gather_kernel(
    gate_hbm, idx_hbm, acts_hbm, grad_ref, w_hbm,
    act_out, logit_out, down_out,
    gate_ref, idx_ref, acts_ref,
    grads, w_buf, acts_send, acts_in, acts_t, hid, hid_sum, back, total,
    in_sem, own_sem, g_recv, z_send, x_send, y_send, c_send,
    h_send, h_recv, b_send, b_recv,
):
    y = lax.axis_index("dp")
    me = lax.axis_index("expert")
    z = lax.div(me, XS * CS)
    x = lax.rem(lax.div(me, CS), XS)
    c = lax.rem(me, CS)
    n_exp = ZS * XS * CS
    n_dev = 2 * n_exp
    top, tok = idx_ref.shape
    routed, width = acts_ref.shape
    half = width // 2
    model = grad_ref.shape[1]
    lid = y * n_exp + me
    own = slot_of(y, x, z, c)

    def dev(yy, ee):
        return {"dp": yy, "expert": ee}

    part_cols = model // PARTS
    own_grads = [
        pltpu.make_async_copy(
            grad_ref.at[:, pl.ds(p * part_cols, part_cols)], grads.at[p, own], own_sem.at[2 + p]
        )
        for p in range(PARTS)
    ]
    for copy in own_grads:
        copy.start()

    barrier = pltpu.get_barrier_semaphore()

    def greet(r, carry):
        other = lax.rem(lid + r, n_dev)
        pl.semaphore_signal(
            barrier, inc=1,
            device_id=dev(lax.div(other, n_exp), lax.rem(other, n_exp)),
            device_id_type=MESH,
        )
        return carry

    lax.fori_loop(1, n_dev, greet, 0)
    loads = [
        pltpu.make_async_copy(src, dst, in_sem.at[at])
        for at, (src, dst) in enumerate(
            ((gate_hbm, gate_ref), (idx_hbm, idx_ref), (acts_hbm, acts_ref), (w_hbm, w_buf))
        )
    ]
    for load in loads:
        load.start()
    for copy in own_grads:
        copy.wait()
    pl.semaphore_wait(barrier, n_dev - 1)

    def grad_copy(p, slot, sem, yy, ee):
        block = grads.at[p, slot]
        return pltpu.make_async_remote_copy(
            src_ref=block, dst_ref=block, send_sem=sem, recv_sem=g_recv.at[p, slot],
            device_id=dev(yy, ee), device_id_type=MESH,
        )

    def arrived(p, slot):
        grad_copy(p, slot, c_send.at[p, 0], y, expert_of(x, z, 1 - c)).wait_recv()

    sent = []

    def send(copy, when=None):
        if when is None:
            copy.start()
        else:
            pl.when(when)(copy.start)
        sent.append((when, copy))

    def pass_on(p, yy, xx, zz, to_x, to_y, when=None):
        slot = slot_of(yy, xx, zz, c)
        in_plane = xx * ZS + zz
        if to_x:
            at = zz if yy is y else ZS
            send(grad_copy(p, slot, x_send.at[p, at], y, expert_of(1 - x, z, c)), when)
        if to_y:
            send(grad_copy(p, slot, y_send.at[p, in_plane], 1 - y, me), when)
        at = yy * XS * ZS + in_plane
        send(grad_copy(p, slot, c_send.at[p, at], y, expert_of(x, z, 1 - c)), when)

    def along_z(p, zz, way, when):
        slot = slot_of(y, x, zz, c)
        sem = z_send.at[p, (way + 1) // 2, zz]
        send(grad_copy(p, slot, sem, y, expert_of(x, z + way, c)), when)

    for p in range(PARTS):
        for way in (1, -1):
            along_z(p, z, way, (z + way >= 0) & (z + way < ZS))
        pass_on(p, y, x, z, True, True)

    for load in loads[:3]:
        load.wait()
    gate = gate_ref[...]
    gate_half = gate.astype(jnp.bfloat16).astype(jnp.float32)
    idx = idx_ref[...].astype(jnp.float32)
    lane = lax.broadcasted_iota(jnp.int32, (tok, routed), 1)
    line = lax.broadcasted_iota(jnp.int32, (tok, routed), 0)
    widen = (lax.div(lane, top) == line).astype(jnp.float32)
    own_row = lax.broadcasted_iota(jnp.int32, (top, routed), 0) == lax.rem(
        lax.broadcasted_iota(jnp.int32, (top, routed), 1), top
    )
    gate_row = jnp.sum(
        jnp.where(own_row, jnp.dot(gate_half, widen, preferred_element_type=jnp.float32), 0.0),
        axis=0, keepdims=True,
    )
    idx_row = jnp.sum(
        jnp.where(own_row, jnp.dot(idx, widen, preferred_element_type=jnp.float32), 0.0),
        axis=0, keepdims=True,
    )
    rows = n_exp * tok
    row = lax.broadcasted_iota(jnp.int32, (rows, routed), 0)
    col = lax.broadcasted_iota(jnp.int32, (rows, routed), 1)
    row_exp = lax.div(row, tok).astype(jnp.float32)
    place = jnp.where(
        (idx_row == row_exp) & (lax.div(col, top) == lax.rem(row, tok)), gate_row, 0.0
    ).astype(jnp.bfloat16)
    weighted = jnp.dot(place, acts_ref[...], preferred_element_type=jnp.float32)
    weighted = weighted.astype(jnp.bfloat16).reshape(n_exp, tok, width)
    acts_send[0] = weighted[:, :, :half]
    acts_send[1] = weighted[:, :, half:]

    tall_row = lax.broadcasted_iota(jnp.int32, (routed, tok), 0)
    tall_col = lax.broadcasted_iota(jnp.int32, (routed, tok), 1)
    spread = (lax.div(tall_row, top) == tall_col).astype(jnp.float32)
    own_k = (
        lax.broadcasted_iota(jnp.int32, (routed, top), 1)
        == lax.rem(lax.broadcasted_iota(jnp.int32, (routed, top), 0), top)
    ).astype(jnp.float32)

    def column(of):
        wide = lax.dot_general(
            spread, of, (((1,), (1,)), ((), ())), preferred_element_type=jnp.float32
        )
        return jnp.sum(wide * own_k, axis=1, keepdims=True)

    gate_col = column(gate_half)
    idx_col = column(idx)
    row = lax.broadcasted_iota(jnp.int32, (routed, rows), 0)
    col = lax.broadcasted_iota(jnp.int32, (routed, rows), 1)
    pick = (
        (idx_col == lax.div(col, tok).astype(jnp.float32))
        & (lax.div(row, top) == lax.rem(col, tok))
    ).astype(jnp.float32).astype(jnp.bfloat16)

    def receive(p, yy, xx, dist, to_z, to_x, to_y):
        for way in (1, -1) if dist else (1,):
            zz = z - way * dist
            there = (zz >= 0) & (zz < ZS) if dist else None
            slot = slot_of(yy, xx, zz, c)
            if dist:
                pl.when(there)(functools.partial(arrived, p, slot))
            else:
                arrived(p, slot)
            if to_z:
                along_z(p, zz, way, there & (z + way >= 0) & (z + way < ZS))
            pass_on(p, yy, xx, zz, to_x, to_y, there)

    def from_z(p, dist):
        receive(p, y, x, dist, True, True, True)

    def from_x(p, dist):
        receive(p, y, 1 - x, dist, False, False, dist != 2)

    def from_group(p, xx, dist):
        receive(p, 1 - y, xx, dist, False, xx is x and dist == 2, False)

    per_half = n_exp // 2
    my_half = lax.div(me, per_half)

    def far_exp(r):
        return (1 - my_half) * per_half + lax.rem(me + r, per_half)

    def near_exp(r):
        return my_half * per_half + lax.rem(me + r, per_half)

    def acts_copy(yy, ee):
        return pltpu.make_async_remote_copy(
            src_ref=acts_send.at[yy, ee], dst_ref=acts_in.at[own],
            send_sem=h_send.at[yy, ee], recv_sem=h_recv.at[own],
            device_id=dev(yy, ee), device_id_type=MESH,
        )

    def acts_far(r, carry):
        acts_copy(y, far_exp(r)).start()
        acts_copy(1 - y, far_exp(r)).start()
        return carry

    def acts_near(r, group):
        acts_copy(group, near_exp(r)).start()
        return group

    own_acts = pltpu.make_async_copy(acts_send.at[y, me], acts_in.at[own], own_sem.at[1])

    def back_copy(ee):
        at = slot_of(0, lax.rem(lax.div(ee, CS), XS), lax.div(ee, XS * CS), lax.rem(ee, CS))
        return pltpu.make_async_remote_copy(
            src_ref=hid.at[at], dst_ref=back.at[me], send_sem=b_send.at[at],
            recv_sem=b_recv.at[me], device_id=dev(y, ee), device_id_type=MESH,
        )

    tile = model // 4

    def hidden(p):
        part = lax.dot_general(
            grads[p, pl.ds(y * n_exp, n_exp)].reshape(n_exp * tok, part_cols),
            w_buf[:, pl.ds(p * part_cols, part_cols)],
            (((1,), (1,)), ((), ())), preferred_element_type=jnp.float32,
        )
        if p:
            part = part + hid_sum[...]
        if p < PARTS - 1:
            hid_sum[...] = part
        else:
            hid[...] = part.astype(jnp.bfloat16).reshape(n_exp, tok, width)

    def mates(p, group):
        for xx in (x, 1 - x):
            for zz in range(ZS):
                arrived(p, slot_of(group, xx, zz, 1 - c))

    parts = range(PARTS)
    for p in parts:
        from_z(p, 1)
    for p in parts:
        from_x(p, 0)
    lax.fori_loop(0, per_half, acts_far, 0)
    for p in parts:
        from_z(p, 2)
    for p in parts:
        from_x(p, 1)
    for p in parts:
        from_z(p, 3)
    for p in parts:
        from_x(p, 2)
    lax.fori_loop(1, per_half, acts_near, y)
    lax.fori_loop(0, per_half, acts_near, 1 - y)
    own_acts.start()
    for dist in range(2):
        for p in parts:
            from_group(p, x, dist)
    loads[3].wait()
    for p in parts:
        from_x(p, 3)
        mates(p, y)
        hidden(p)
    own_back = pltpu.make_async_copy(hid.at[own - y * n_exp], back.at[me], own_sem.at[0])
    own_back.start()

    for r in range(per_half):
        back_copy(far_exp(r)).start()
    for r in range(1, per_half):
        back_copy(near_exp(r)).start()

    def acts_wait(r, group):
        ee = lax.rem(me + r, n_exp)
        slot = slot_of(
            group, lax.rem(lax.div(ee, CS), XS), lax.div(ee, XS * CS), lax.rem(ee, CS)
        )
        pltpu.make_async_remote_copy(
            src_ref=acts_send.at[0, 0], dst_ref=acts_in.at[slot],
            send_sem=h_send.at[0, 0], recv_sem=h_recv.at[slot],
            device_id=dev(1 - y, me), device_id_type=MESH,
        ).wait_recv()
        return group

    def turn(group, at):
        rows_in = acts_in[pl.ds(group * n_exp, n_exp)].reshape(n_exp * tok, half)
        acts_t[at] = rows_in.T

    def down_part(group, at, n):
        p = lax.div(n * tile, part_cols)
        cols = pl.ds(pl.multiple_of(lax.rem(n * tile, part_cols), tile), tile)
        return jnp.dot(
            acts_t[at], grads[p, pl.ds(group * n_exp, n_exp), :, cols].reshape(n_exp * tok, tile),
            preferred_element_type=jnp.float32,
        )

    for dist in range(2, ZS):
        for p in parts:
            from_group(p, x, dist)

    for dist in range(ZS):
        for p in parts:
            from_group(p, 1 - x, dist)

    lax.fori_loop(1, n_exp, acts_wait, y)
    own_acts.wait()
    turn(y, 0)

    @pl.loop(0, model // tile)
    def _(n):
        cols = pl.ds(pl.multiple_of(n * tile, tile), tile)
        total[:, cols] = down_part(y, 0, n)

    lax.fori_loop(0, n_exp, acts_wait, 1 - y)
    turn(1 - y, 1)
    for p in parts:
        mates(p, 1 - y)

    @pl.loop(0, model // tile)
    def _(n):
        cols = pl.ds(pl.multiple_of(n * tile, tile), tile)
        down_out[:, cols] = (total[:, cols] + down_part(1 - y, 1, n)).astype(jnp.bfloat16)

    for when, copy in sent:
        if when is None:
            copy.wait_send()
        else:
            pl.when(when)(copy.wait_send)

    def acts_sent(r, group):
        acts_copy(group, lax.rem(me + r, n_exp)).wait_send()
        return group

    lax.fori_loop(1, n_exp, acts_sent, y)
    lax.fori_loop(0, n_exp, acts_sent, 1 - y)
    for r in range(1, n_exp):
        back_copy(lax.rem(me + r, n_exp)).wait_send()

    def back_wait(r, carry):
        ee = lax.rem(me + r, n_exp)
        pltpu.make_async_remote_copy(
            src_ref=hid.at[0], dst_ref=back.at[ee],
            send_sem=b_send.at[0], recv_sem=b_recv.at[ee],
            device_id=dev(1 - y, me), device_id_type=MESH,
        ).wait_recv()
        return carry

    lax.fori_loop(1, n_exp, back_wait, 0)
    own_back.wait()
    picked = jnp.dot(pick, back[...].reshape(rows, width), preferred_element_type=jnp.float32)
    act_out[...] = (gate_col * picked).astype(jnp.bfloat16)
    score = jnp.sum(picked * acts_ref[...].astype(jnp.float32), axis=1, keepdims=True)
    score = score.astype(jnp.bfloat16).astype(jnp.float32)
    score = jnp.dot(own_row.astype(jnp.float32), score * spread, preferred_element_type=jnp.float32)
    logit_out[...] = gate * (score - jnp.sum(gate * score, axis=0, keepdims=True))


def store_kernel(*refs):
    results, outs, sems = refs[:3], refs[3:6], refs[6]
    copies = []
    for src, dst in zip(results, outs):
        rows = src.shape[0]
        step = rows // STRIPS if rows % (16 * STRIPS) == 0 else rows
        for at in range(0, rows, step):
            strip = pl.ds(at, step)
            copies.append(
                pltpu.make_async_copy(src.at[strip], dst.at[strip], sems.at[len(copies)])
            )
    for copy in copies[::-1]:
        copy.start()
    for copy in copies:
        copy.wait()


def gathered_shards(out_grad, hidden_acts, gate_weights, expert_idx, down_weight):
    tok, top = expert_idx.shape
    model = out_grad.shape[1]
    width = hidden_acts.shape[2]
    half = width // 2
    n_exp = ZS * XS * CS
    n_dev = 2 * n_exp
    dma = pltpu.SemaphoreType.DMA
    vmem = pl.BlockSpec(memory_space=pltpu.VMEM)
    hbm = pl.BlockSpec(memory_space=pltpu.HBM)
    act, logit, down = pl.pallas_call(
        gather_kernel,
        out_shape=(
            jax.ShapeDtypeStruct((tok * top, width), jnp.bfloat16),
            jax.ShapeDtypeStruct((top, tok), jnp.float32),
            jax.ShapeDtypeStruct((half, model), jnp.bfloat16),
        ),
        in_specs=[hbm] * 5,
        out_specs=(vmem, vmem, vmem),
        scratch_shapes=[
            pltpu.VMEM((top, tok), jnp.float32),
            pltpu.VMEM((top, tok), jnp.int32),
            pltpu.VMEM((tok * top, width), jnp.bfloat16),
            pltpu.VMEM((PARTS, n_dev, tok, model // PARTS), jnp.bfloat16),
            pltpu.VMEM((width, model), jnp.bfloat16),
            pltpu.VMEM((2, n_exp, tok, half), jnp.bfloat16),
            pltpu.VMEM((n_dev, tok, half), jnp.bfloat16),
            pltpu.VMEM((2, half, n_exp * tok), jnp.bfloat16),
            pltpu.VMEM((n_exp, tok, width), jnp.bfloat16),
            pltpu.VMEM((n_exp * tok, width), jnp.float32),
            pltpu.VMEM((n_exp, tok, width), jnp.bfloat16),
            pltpu.VMEM((half, model), jnp.float32),
            dma((4,)),
            dma((2 + PARTS,)),
            dma((PARTS, n_dev)),
            dma((PARTS, 2, ZS)),
            dma((PARTS, ZS + 1)),
            dma((PARTS, XS * ZS)),
            dma((PARTS, 2 * XS * ZS)),
            dma((2, n_exp)),
            dma((n_dev,)),
            dma((n_exp,)),
            dma((n_exp,)),
        ],
        compiler_params=pltpu.CompilerParams(
            collective_id=0, has_side_effects=True, vmem_limit_bytes=36 * 1024 * 1024
        ),
        cost_estimate=pl.CostEstimate(
            flops=6 * n_exp * tok * model * width, bytes_accessed=3 * width * model * 2,
            transcendentals=0,
        ),
    )(
        *(
            pltpu.with_memory_space_constraint(array, pltpu.HBM)
            for array in (
                gate_weights.T, expert_idx.T, hidden_acts.reshape(tok * top, width), out_grad,
                down_weight.reshape(width, model),
            )
        )
    )
    results = (act, logit, down)
    act, logit, down = pl.pallas_call(
        store_kernel,
        out_shape=tuple(jax.ShapeDtypeStruct(of.shape, of.dtype) for of in results),
        in_specs=[vmem] * 3,
        out_specs=(hbm,) * 3,
        scratch_shapes=[dma((3 * STRIPS,))],
        compiler_params=pltpu.CompilerParams(vmem_limit_bytes=16 * 1024 * 1024),
    )(*results)
    return act.reshape(tok, top, width), logit.T, down[None]


def solution(mesh):
    gathered = mesh.shape["dp"] == 2 and mesh.shape["expert"] == ZS * XS * CS
    return jax.shard_map(
        gathered_shards if gathered else routed_shards,
        mesh=mesh,
        in_specs=(
            P(("dp", "expert"), None),
            P(("dp", "expert"), None, None),
            P(("dp", "expert"), None),
            P(("dp", "expert"), None),
            P("expert", None, None),
        ),
        out_specs=(
            P(("dp", "expert"), None, None),
            P(("dp", "expert"), None),
            P("expert", "dp", None),
        ),
        check_vma=False,
    )
```

```python
import functools

import jax
import jax.numpy as jnp
from jax import lax
from jax.experimental import pallas as pl
from jax.experimental.pallas import tpu as pltpu
from jax.sharding import PartitionSpec as P

MESH = pl.DeviceIdType.MESH
ZS, XS, CS = 4, 2, 2
STRIPS = 4
PARTS = 2


def routed_shards(out_grad, hidden_acts, gate_weights, expert_idx, down_weight):
    tok_rows, top_count = expert_idx.shape
    routed = tok_rows * top_count
    hidden_width = hidden_acts.shape[2]
    owners = lax.axis_size("expert")
    experts = owners * down_weight.shape[0]
    capacity = min(tok_rows, max(2, (3 * tok_rows * top_count + 2 * experts - 1) // (2 * experts)))
    slot_count = experts * capacity
    flat_expert = expert_idx.reshape(routed)
    member = (flat_expert[:, None] == jnp.arange(experts, dtype=jnp.int32)[None, :]).astype(
        jnp.bfloat16
    )
    row_line = jnp.arange(routed, dtype=jnp.int32)
    earlier_mask = (row_line[:, None] > row_line[None, :]).astype(jnp.bfloat16)
    earlier = jnp.dot(earlier_mask, member, preferred_element_type=jnp.float32)
    position = jnp.sum(earlier * member.astype(jnp.float32), axis=1).astype(jnp.int32)
    slot_index = flat_expert * capacity + position
    placement = (jnp.arange(slot_count, dtype=jnp.int32)[:, None] == slot_index[None, :]).astype(
        jnp.bfloat16
    )
    token_place = jnp.sum(placement.reshape(slot_count, tok_rows, top_count), axis=2)
    gate_half = lax.optimization_barrier(gate_weights.astype(jnp.bfloat16))
    send_grads = jnp.dot(token_place, out_grad, preferred_element_type=jnp.float32).astype(
        jnp.bfloat16
    )
    send_acts = jnp.dot(
        placement, hidden_acts.reshape(routed, hidden_width), preferred_element_type=jnp.float32
    ).astype(jnp.bfloat16)
    send_gate = jnp.dot(
        placement, gate_half.reshape(routed, 1), preferred_element_type=jnp.float32
    ).astype(jnp.bfloat16)
    grads_in, acts_in, gate_in = (
        lax.all_to_all(
            send_grads.reshape(owners, capacity, out_grad.shape[1]),
            "expert",
            split_axis=0,
            concat_axis=0,
            tiled=True,
        ),
        lax.all_to_all(
            send_acts.reshape(owners, capacity, hidden_width),
            "expert",
            split_axis=0,
            concat_axis=0,
            tiled=True,
        ),
        lax.all_to_all(
            send_gate.reshape(owners, capacity), "expert", split_axis=0, concat_axis=0, tiled=True
        ),
    )
    grads_in = grads_in.reshape(slot_count, out_grad.shape[1])
    acts_in = acts_in.reshape(slot_count, hidden_width)
    gate_rows = gate_in.reshape(slot_count, 1).astype(jnp.float32)
    expert_weight = down_weight[0]
    grad_hidden = lax.dot_general(
        grads_in, expert_weight, (((1,), (1,)), ((), ())), preferred_element_type=jnp.float32
    )
    act_back = (gate_rows * grad_hidden).astype(jnp.bfloat16)
    score_back = jnp.sum(grad_hidden * acts_in.astype(jnp.float32), axis=1).astype(jnp.bfloat16)
    scaled_grad = (gate_rows * grads_in.astype(jnp.float32)).astype(jnp.bfloat16)
    back_rows, back_scores = (
        lax.all_to_all(
            act_back.reshape(owners, capacity, hidden_width),
            "expert",
            split_axis=0,
            concat_axis=0,
            tiled=True,
        ),
        lax.all_to_all(
            score_back.reshape(owners, capacity), "expert", split_axis=0, concat_axis=0, tiled=True
        ),
    )
    weight_term = lax.dot_general(
        acts_in, scaled_grad, (((0,), (0,)), ((), ())), preferred_element_type=jnp.float32
    )
    summed = lax.psum_scatter(
        weight_term.astype(jnp.bfloat16), "dp", scatter_dimension=0, tiled=True
    )
    down_grad = summed[None]
    act_grad = lax.dot_general(
        placement,
        back_rows.reshape(slot_count, hidden_width),
        (((0,), (0,)), ((), ())),
        preferred_element_type=jnp.float32,
    ).astype(jnp.bfloat16)
    score_tok = lax.dot_general(
        placement,
        back_scores.reshape(slot_count, 1),
        (((0,), (0,)), ((), ())),
        preferred_element_type=jnp.float32,
    ).reshape(tok_rows, top_count)
    logit_grad = gate_weights * (
        score_tok - jnp.sum(gate_weights * score_tok, axis=1, keepdims=True)
    )
    return (act_grad.reshape(tok_rows, top_count, hidden_width), logit_grad, down_grad)


def slot_of(y, x, z, c):
    return y * (XS * ZS * CS) + x * (ZS * CS) + z * CS + c


def expert_of(x, z, c):
    return z * (XS * CS) + x * CS + c


def gather_kernel(
    gate_hbm, idx_hbm, acts_hbm, grad_ref, w_hbm,
    act_out, logit_out, down_out,
    gate_ref, idx_ref, acts_ref,
    grads, w_buf, acts_send, acts_in, acts_t, hid, hid_sum, back, total,
    in_sem, own_sem, g_recv, z_send, x_send, y_send, c_send,
    h_send, h_recv, b_send, b_recv,
):
    y = lax.axis_index("dp")
    me = lax.axis_index("expert")
    z = lax.div(me, XS * CS)
    x = lax.rem(lax.div(me, CS), XS)
    c = lax.rem(me, CS)
    n_exp = ZS * XS * CS
    n_dev = 2 * n_exp
    top, tok = idx_ref.shape
    routed, width = acts_ref.shape
    half = width // 2
    model = grad_ref.shape[1]
    lid = y * n_exp + me
    own = slot_of(y, x, z, c)

    def dev(yy, ee):
        return {"dp": yy, "expert": ee}

    part_cols = model // PARTS
    own_grads = [
        pltpu.make_async_copy(
            grad_ref.at[:, pl.ds(p * part_cols, part_cols)], grads.at[p, own], own_sem.at[2 + p]
        )
        for p in range(PARTS)
    ]
    for copy in own_grads:
        copy.start()

    barrier = pltpu.get_barrier_semaphore()

    def greet(r, carry):
        other = lax.rem(lid + r, n_dev)
        pl.semaphore_signal(
            barrier, inc=1,
            device_id=dev(lax.div(other, n_exp), lax.rem(other, n_exp)),
            device_id_type=MESH,
        )
        return carry

    lax.fori_loop(1, n_dev, greet, 0)
    loads = [
        pltpu.make_async_copy(src, dst, in_sem.at[at])
        for at, (src, dst) in enumerate(
            ((gate_hbm, gate_ref), (idx_hbm, idx_ref), (acts_hbm, acts_ref), (w_hbm, w_buf))
        )
    ]
    for load in loads:
        load.start()
    for copy in own_grads:
        copy.wait()
    pl.semaphore_wait(barrier, n_dev - 1)

    def grad_copy(p, slot, sem, yy, ee):
        block = grads.at[p, slot]
        return pltpu.make_async_remote_copy(
            src_ref=block, dst_ref=block, send_sem=sem, recv_sem=g_recv.at[p, slot],
            device_id=dev(yy, ee), device_id_type=MESH,
        )

    def arrived(p, slot):
        grad_copy(p, slot, c_send.at[p, 0], y, expert_of(x, z, 1 - c)).wait_recv()

    sent = []

    def send(copy, when=None):
        if when is None:
            copy.start()
        else:
            pl.when(when)(copy.start)
        sent.append((when, copy))

    def pass_on(p, yy, xx, zz, to_x, to_y, when=None):
        slot = slot_of(yy, xx, zz, c)
        in_plane = xx * ZS + zz
        if to_x:
            at = zz if yy is y else ZS
            send(grad_copy(p, slot, x_send.at[p, at], y, expert_of(1 - x, z, c)), when)
        at = yy * XS * ZS + in_plane
        send(grad_copy(p, slot, c_send.at[p, at], y, expert_of(x, z, 1 - c)), when)
        if to_y:
            send(grad_copy(p, slot, y_send.at[p, in_plane], 1 - y, me), when)

    def along_z(p, zz, way, when):
        slot = slot_of(y, x, zz, c)
        sem = z_send.at[p, (way + 1) // 2, zz]
        send(grad_copy(p, slot, sem, y, expert_of(x, z + way, c)), when)

    for p in range(PARTS):
        for way in (1, -1):
            along_z(p, z, way, (z + way >= 0) & (z + way < ZS))
        pass_on(p, y, x, z, True, True)

    for load in loads[:3]:
        load.wait()
    gate = gate_ref[...]
    gate_half = gate.astype(jnp.bfloat16).astype(jnp.float32)
    idx = idx_ref[...].astype(jnp.float32)
    lane = lax.broadcasted_iota(jnp.int32, (tok, routed), 1)
    line = lax.broadcasted_iota(jnp.int32, (tok, routed), 0)
    widen = (lax.div(lane, top) == line).astype(jnp.float32)
    own_row = lax.broadcasted_iota(jnp.int32, (top, routed), 0) == lax.rem(
        lax.broadcasted_iota(jnp.int32, (top, routed), 1), top
    )
    gate_row = jnp.sum(
        jnp.where(own_row, jnp.dot(gate_half, widen, preferred_element_type=jnp.float32), 0.0),
        axis=0, keepdims=True,
    )
    idx_row = jnp.sum(
        jnp.where(own_row, jnp.dot(idx, widen, preferred_element_type=jnp.float32), 0.0),
        axis=0, keepdims=True,
    )
    rows = n_exp * tok
    row = lax.broadcasted_iota(jnp.int32, (rows, routed), 0)
    col = lax.broadcasted_iota(jnp.int32, (rows, routed), 1)
    row_exp = lax.div(row, tok).astype(jnp.float32)
    place = jnp.where(
        (idx_row == row_exp) & (lax.div(col, top) == lax.rem(row, tok)), gate_row, 0.0
    ).astype(jnp.bfloat16)
    weighted = jnp.dot(place, acts_ref[...], preferred_element_type=jnp.float32)
    weighted = weighted.astype(jnp.bfloat16).reshape(n_exp, tok, width)
    acts_send[0] = weighted[:, :, :half]
    acts_send[1] = weighted[:, :, half:]

    tall_row = lax.broadcasted_iota(jnp.int32, (routed, tok), 0)
    tall_col = lax.broadcasted_iota(jnp.int32, (routed, tok), 1)
    spread = (lax.div(tall_row, top) == tall_col).astype(jnp.float32)
    own_k = (
        lax.broadcasted_iota(jnp.int32, (routed, top), 1)
        == lax.rem(lax.broadcasted_iota(jnp.int32, (routed, top), 0), top)
    ).astype(jnp.float32)

    def column(of):
        wide = lax.dot_general(
            spread, of, (((1,), (1,)), ((), ())), preferred_element_type=jnp.float32
        )
        return jnp.sum(wide * own_k, axis=1, keepdims=True)

    gate_col = column(gate_half)
    idx_col = column(idx)
    row = lax.broadcasted_iota(jnp.int32, (routed, rows), 0)
    col = lax.broadcasted_iota(jnp.int32, (routed, rows), 1)
    pick = (
        (idx_col == lax.div(col, tok).astype(jnp.float32))
        & (lax.div(row, top) == lax.rem(col, tok))
    ).astype(jnp.float32).astype(jnp.bfloat16)

    def receive(p, yy, xx, dist, to_z, to_x, to_y):
        for way in (1, -1) if dist else (1,):
            zz = z - way * dist
            there = (zz >= 0) & (zz < ZS) if dist else None
            slot = slot_of(yy, xx, zz, c)
            if dist:
                pl.when(there)(functools.partial(arrived, p, slot))
            else:
                arrived(p, slot)
            if to_z:
                along_z(p, zz, way, there & (z + way >= 0) & (z + way < ZS))
            pass_on(p, yy, xx, zz, to_x, to_y, there)

    def from_z(p, dist):
        receive(p, y, x, dist, True, True, True)

    def from_x(p, dist):
        receive(p, y, 1 - x, dist, False, False, dist != 2)

    def from_group(p, xx, dist):
        receive(p, 1 - y, xx, dist, False, xx is x and dist == 2, False)

    def acts_copy(yy, ee):
        return pltpu.make_async_remote_copy(
            src_ref=acts_send.at[yy, ee], dst_ref=acts_in.at[own],
            send_sem=h_send.at[yy, ee], recv_sem=h_recv.at[own],
            device_id=dev(yy, ee), device_id_type=MESH,
        )

    inner = (z > 0) & (z < ZS - 1)
    per_z = XS * CS

    def acts_early(r, carry):
        ee = (ZS - 1 - z) * per_z + lax.rem(me + r, per_z)
        acts_copy(y, ee).start()
        acts_copy(1 - y, ee).start()
        return carry

    def acts_late(r, carry):
        ee = lax.rem(me + r, n_exp)
        waits = jnp.logical_not(inner & (lax.div(ee, per_z) == ZS - 1 - z))

        @pl.when(waits & (r > 0))
        def _():
            acts_copy(y, ee).start()

        @pl.when(waits)
        def _():
            acts_copy(1 - y, ee).start()

        return carry

    own_acts = pltpu.make_async_copy(acts_send.at[y, me], acts_in.at[own], own_sem.at[1])

    def back_copy(ee):
        at = slot_of(0, lax.rem(lax.div(ee, CS), XS), lax.div(ee, XS * CS), lax.rem(ee, CS))
        return pltpu.make_async_remote_copy(
            src_ref=hid.at[at], dst_ref=back.at[me], send_sem=b_send.at[at],
            recv_sem=b_recv.at[me], device_id=dev(y, ee), device_id_type=MESH,
        )

    tile = model // 4

    def hidden(p):
        part = lax.dot_general(
            grads[p, pl.ds(y * n_exp, n_exp)].reshape(n_exp * tok, part_cols),
            w_buf[:, pl.ds(p * part_cols, part_cols)],
            (((1,), (1,)), ((), ())), preferred_element_type=jnp.float32,
        )
        if p:
            part = part + hid_sum[...]
        if p < PARTS - 1:
            hid_sum[...] = part
        else:
            hid[...] = part.astype(jnp.bfloat16).reshape(n_exp, tok, width)

    def mates(p, group):
        for xx in (x, 1 - x):
            for zz in range(ZS):
                arrived(p, slot_of(group, xx, zz, 1 - c))

    parts = range(PARTS)
    for p in parts:
        from_z(p, 1)
    for p in parts:
        from_x(p, 0)

    @pl.when(inner)
    def _():
        lax.fori_loop(0, per_z, acts_early, 0)

    for p in parts:
        from_z(p, 2)
    for p in parts:
        from_x(p, 1)
    for p in parts:
        from_z(p, 3)
    for p in parts:
        from_x(p, 2)
    lax.fori_loop(0, n_exp, acts_late, 0)
    own_acts.start()
    for dist in range(2):
        for p in parts:
            from_group(p, x, dist)
    loads[3].wait()
    for p in parts:
        from_x(p, 3)
        mates(p, y)
        hidden(p)
    own_back = pltpu.make_async_copy(hid.at[own - y * n_exp], back.at[me], own_sem.at[0])
    own_back.start()

    for r in range(1, n_exp):
        back_copy(lax.rem(me + r, n_exp)).start()

    def acts_wait(r, group):
        ee = lax.rem(me + r, n_exp)
        slot = slot_of(
            group, lax.rem(lax.div(ee, CS), XS), lax.div(ee, XS * CS), lax.rem(ee, CS)
        )
        pltpu.make_async_remote_copy(
            src_ref=acts_send.at[0, 0], dst_ref=acts_in.at[slot],
            send_sem=h_send.at[0, 0], recv_sem=h_recv.at[slot],
            device_id=dev(1 - y, me), device_id_type=MESH,
        ).wait_recv()
        return group

    def turn(group, at):
        rows_in = acts_in[pl.ds(group * n_exp, n_exp)].reshape(n_exp * tok, half)
        acts_t[at] = rows_in.T

    def down_part(group, at, n):
        p = lax.div(n * tile, part_cols)
        cols = pl.ds(pl.multiple_of(lax.rem(n * tile, part_cols), tile), tile)
        return jnp.dot(
            acts_t[at], grads[p, pl.ds(group * n_exp, n_exp), :, cols].reshape(n_exp * tok, tile),
            preferred_element_type=jnp.float32,
        )

    for dist in range(2, ZS):
        for p in parts:
            from_group(p, x, dist)

    for dist in range(ZS):
        for p in parts:
            from_group(p, 1 - x, dist)

    lax.fori_loop(1, n_exp, acts_wait, y)
    own_acts.wait()
    turn(y, 0)

    @pl.loop(0, model // tile)
    def _(n):
        cols = pl.ds(pl.multiple_of(n * tile, tile), tile)
        total[:, cols] = down_part(y, 0, n)

    lax.fori_loop(0, n_exp, acts_wait, 1 - y)
    turn(1 - y, 1)
    for p in parts:
        mates(p, 1 - y)

    @pl.loop(0, model // tile)
    def _(n):
        cols = pl.ds(pl.multiple_of(n * tile, tile), tile)
        down_out[:, cols] = (total[:, cols] + down_part(1 - y, 1, n)).astype(jnp.bfloat16)

    for when, copy in sent:
        if when is None:
            copy.wait_send()
        else:
            pl.when(when)(copy.wait_send)

    def acts_sent(r, group):
        acts_copy(group, lax.rem(me + r, n_exp)).wait_send()
        return group

    lax.fori_loop(1, n_exp, acts_sent, y)
    lax.fori_loop(0, n_exp, acts_sent, 1 - y)
    for r in range(1, n_exp):
        back_copy(lax.rem(me + r, n_exp)).wait_send()

    def back_wait(r, carry):
        ee = lax.rem(me + r, n_exp)
        pltpu.make_async_remote_copy(
            src_ref=hid.at[0], dst_ref=back.at[ee],
            send_sem=b_send.at[0], recv_sem=b_recv.at[ee],
            device_id=dev(1 - y, me), device_id_type=MESH,
        ).wait_recv()
        return carry

    lax.fori_loop(1, n_exp, back_wait, 0)
    own_back.wait()
    picked = jnp.dot(pick, back[...].reshape(rows, width), preferred_element_type=jnp.float32)
    act_out[...] = (gate_col * picked).astype(jnp.bfloat16)
    score = jnp.sum(picked * acts_ref[...].astype(jnp.float32), axis=1, keepdims=True)
    score = score.astype(jnp.bfloat16).astype(jnp.float32)
    score = jnp.dot(own_row.astype(jnp.float32), score * spread, preferred_element_type=jnp.float32)
    logit_out[...] = gate * (score - jnp.sum(gate * score, axis=0, keepdims=True))


def store_kernel(*refs):
    results, outs, sems = refs[:3], refs[3:6], refs[6]
    copies = []
    for src, dst in zip(results, outs):
        rows = src.shape[0]
        step = rows // STRIPS if rows % (16 * STRIPS) == 0 else rows
        for at in range(0, rows, step):
            strip = pl.ds(at, step)
            copies.append(
                pltpu.make_async_copy(src.at[strip], dst.at[strip], sems.at[len(copies)])
            )
    for copy in copies[::-1]:
        copy.start()
    for copy in copies:
        copy.wait()


def gathered_shards(out_grad, hidden_acts, gate_weights, expert_idx, down_weight):
    tok, top = expert_idx.shape
    model = out_grad.shape[1]
    width = hidden_acts.shape[2]
    half = width // 2
    n_exp = ZS * XS * CS
    n_dev = 2 * n_exp
    dma = pltpu.SemaphoreType.DMA
    vmem = pl.BlockSpec(memory_space=pltpu.VMEM)
    hbm = pl.BlockSpec(memory_space=pltpu.HBM)
    act, logit, down = pl.pallas_call(
        gather_kernel,
        out_shape=(
            jax.ShapeDtypeStruct((tok * top, width), jnp.bfloat16),
            jax.ShapeDtypeStruct((top, tok), jnp.float32),
            jax.ShapeDtypeStruct((half, model), jnp.bfloat16),
        ),
        in_specs=[hbm] * 5,
        out_specs=(vmem, vmem, vmem),
        scratch_shapes=[
            pltpu.VMEM((top, tok), jnp.float32),
            pltpu.VMEM((top, tok), jnp.int32),
            pltpu.VMEM((tok * top, width), jnp.bfloat16),
            pltpu.VMEM((PARTS, n_dev, tok, model // PARTS), jnp.bfloat16),
            pltpu.VMEM((width, model), jnp.bfloat16),
            pltpu.VMEM((2, n_exp, tok, half), jnp.bfloat16),
            pltpu.VMEM((n_dev, tok, half), jnp.bfloat16),
            pltpu.VMEM((2, half, n_exp * tok), jnp.bfloat16),
            pltpu.VMEM((n_exp, tok, width), jnp.bfloat16),
            pltpu.VMEM((n_exp * tok, width), jnp.float32),
            pltpu.VMEM((n_exp, tok, width), jnp.bfloat16),
            pltpu.VMEM((half, model), jnp.float32),
            dma((4,)),
            dma((2 + PARTS,)),
            dma((PARTS, n_dev)),
            dma((PARTS, 2, ZS)),
            dma((PARTS, ZS + 1)),
            dma((PARTS, XS * ZS)),
            dma((PARTS, 2 * XS * ZS)),
            dma((2, n_exp)),
            dma((n_dev,)),
            dma((n_exp,)),
            dma((n_exp,)),
        ],
        compiler_params=pltpu.CompilerParams(
            collective_id=0, has_side_effects=True, vmem_limit_bytes=36 * 1024 * 1024
        ),
        cost_estimate=pl.CostEstimate(
            flops=6 * n_exp * tok * model * width, bytes_accessed=3 * width * model * 2,
            transcendentals=0,
        ),
    )(
        *(
            pltpu.with_memory_space_constraint(array, pltpu.HBM)
            for array in (
                gate_weights.T, expert_idx.T, hidden_acts.reshape(tok * top, width), out_grad,
                down_weight.reshape(width, model),
            )
        )
    )
    results = (act, logit, down)
    act, logit, down = pl.pallas_call(
        store_kernel,
        out_shape=tuple(jax.ShapeDtypeStruct(of.shape, of.dtype) for of in results),
        in_specs=[vmem] * 3,
        out_specs=(hbm,) * 3,
        scratch_shapes=[dma((3 * STRIPS,))],
        compiler_params=pltpu.CompilerParams(vmem_limit_bytes=16 * 1024 * 1024),
    )(*results)
    return act.reshape(tok, top, width), logit.T, down[None]


def solution(mesh):
    gathered = mesh.shape["dp"] == 2 and mesh.shape["expert"] == ZS * XS * CS
    return jax.shard_map(
        gathered_shards if gathered else routed_shards,
        mesh=mesh,
        in_specs=(
            P(("dp", "expert"), None),
            P(("dp", "expert"), None, None),
            P(("dp", "expert"), None),
            P(("dp", "expert"), None),
            P("expert", None, None),
        ),
        out_specs=(
            P(("dp", "expert"), None, None),
            P(("dp", "expert"), None),
            P("expert", "dp", None),
        ),
        check_vma=False,
    )
```

```python
import functools

import jax
import jax.numpy as jnp
from jax import lax
from jax.experimental import pallas as pl
from jax.experimental.pallas import tpu as pltpu
from jax.sharding import PartitionSpec as P

MESH = pl.DeviceIdType.MESH
ZS, XS, CS = 4, 2, 2
STRIPS = 4
PARTS = 2


def routed_shards(out_grad, hidden_acts, gate_weights, expert_idx, down_weight):
    tok_rows, top_count = expert_idx.shape
    routed = tok_rows * top_count
    hidden_width = hidden_acts.shape[2]
    owners = lax.axis_size("expert")
    experts = owners * down_weight.shape[0]
    capacity = min(tok_rows, max(2, (3 * tok_rows * top_count + 2 * experts - 1) // (2 * experts)))
    slot_count = experts * capacity
    flat_expert = expert_idx.reshape(routed)
    member = (flat_expert[:, None] == jnp.arange(experts, dtype=jnp.int32)[None, :]).astype(
        jnp.bfloat16
    )
    row_line = jnp.arange(routed, dtype=jnp.int32)
    earlier_mask = (row_line[:, None] > row_line[None, :]).astype(jnp.bfloat16)
    earlier = jnp.dot(earlier_mask, member, preferred_element_type=jnp.float32)
    position = jnp.sum(earlier * member.astype(jnp.float32), axis=1).astype(jnp.int32)
    slot_index = flat_expert * capacity + position
    placement = (jnp.arange(slot_count, dtype=jnp.int32)[:, None] == slot_index[None, :]).astype(
        jnp.bfloat16
    )
    token_place = jnp.sum(placement.reshape(slot_count, tok_rows, top_count), axis=2)
    gate_half = lax.optimization_barrier(gate_weights.astype(jnp.bfloat16))
    send_grads = jnp.dot(token_place, out_grad, preferred_element_type=jnp.float32).astype(
        jnp.bfloat16
    )
    send_acts = jnp.dot(
        placement, hidden_acts.reshape(routed, hidden_width), preferred_element_type=jnp.float32
    ).astype(jnp.bfloat16)
    send_gate = jnp.dot(
        placement, gate_half.reshape(routed, 1), preferred_element_type=jnp.float32
    ).astype(jnp.bfloat16)
    grads_in, acts_in, gate_in = (
        lax.all_to_all(
            send_grads.reshape(owners, capacity, out_grad.shape[1]),
            "expert",
            split_axis=0,
            concat_axis=0,
            tiled=True,
        ),
        lax.all_to_all(
            send_acts.reshape(owners, capacity, hidden_width),
            "expert",
            split_axis=0,
            concat_axis=0,
            tiled=True,
        ),
        lax.all_to_all(
            send_gate.reshape(owners, capacity), "expert", split_axis=0, concat_axis=0, tiled=True
        ),
    )
    grads_in = grads_in.reshape(slot_count, out_grad.shape[1])
    acts_in = acts_in.reshape(slot_count, hidden_width)
    gate_rows = gate_in.reshape(slot_count, 1).astype(jnp.float32)
    expert_weight = down_weight[0]
    grad_hidden = lax.dot_general(
        grads_in, expert_weight, (((1,), (1,)), ((), ())), preferred_element_type=jnp.float32
    )
    act_back = (gate_rows * grad_hidden).astype(jnp.bfloat16)
    score_back = jnp.sum(grad_hidden * acts_in.astype(jnp.float32), axis=1).astype(jnp.bfloat16)
    scaled_grad = (gate_rows * grads_in.astype(jnp.float32)).astype(jnp.bfloat16)
    back_rows, back_scores = (
        lax.all_to_all(
            act_back.reshape(owners, capacity, hidden_width),
            "expert",
            split_axis=0,
            concat_axis=0,
            tiled=True,
        ),
        lax.all_to_all(
            score_back.reshape(owners, capacity), "expert", split_axis=0, concat_axis=0, tiled=True
        ),
    )
    weight_term = lax.dot_general(
        acts_in, scaled_grad, (((0,), (0,)), ((), ())), preferred_element_type=jnp.float32
    )
    summed = lax.psum_scatter(
        weight_term.astype(jnp.bfloat16), "dp", scatter_dimension=0, tiled=True
    )
    down_grad = summed[None]
    act_grad = lax.dot_general(
        placement,
        back_rows.reshape(slot_count, hidden_width),
        (((0,), (0,)), ((), ())),
        preferred_element_type=jnp.float32,
    ).astype(jnp.bfloat16)
    score_tok = lax.dot_general(
        placement,
        back_scores.reshape(slot_count, 1),
        (((0,), (0,)), ((), ())),
        preferred_element_type=jnp.float32,
    ).reshape(tok_rows, top_count)
    logit_grad = gate_weights * (
        score_tok - jnp.sum(gate_weights * score_tok, axis=1, keepdims=True)
    )
    return (act_grad.reshape(tok_rows, top_count, hidden_width), logit_grad, down_grad)


def slot_of(y, x, z, c):
    return y * (XS * ZS * CS) + x * (ZS * CS) + z * CS + c


def expert_of(x, z, c):
    return z * (XS * CS) + x * CS + c


def gather_kernel(
    gate_hbm, idx_hbm, acts_hbm, grad_ref, w_hbm,
    act_out, logit_out, down_out,
    gate_ref, idx_ref, acts_ref,
    grads, w_buf, acts_send, acts_in, acts_t, hid, hid_sum, back, total,
    in_sem, own_sem, g_recv, z_send, x_send, y_send, c_send,
    h_send, h_recv, b_send, b_recv,
):
    y = lax.axis_index("dp")
    me = lax.axis_index("expert")
    z = lax.div(me, XS * CS)
    x = lax.rem(lax.div(me, CS), XS)
    c = lax.rem(me, CS)
    n_exp = ZS * XS * CS
    n_dev = 2 * n_exp
    top, tok = idx_ref.shape
    routed, width = acts_ref.shape
    half = width // 2
    model = grad_ref.shape[1]
    lid = y * n_exp + me
    own = slot_of(y, x, z, c)

    def dev(yy, ee):
        return {"dp": yy, "expert": ee}

    part_cols = model // PARTS
    own_grads = [
        pltpu.make_async_copy(
            grad_ref.at[:, pl.ds(p * part_cols, part_cols)], grads.at[p, own], own_sem.at[2 + p]
        )
        for p in range(PARTS)
    ]
    for copy in own_grads:
        copy.start()

    barrier = pltpu.get_barrier_semaphore()

    def greet(r, carry):
        other = lax.rem(lid + r, n_dev)
        pl.semaphore_signal(
            barrier, inc=1,
            device_id=dev(lax.div(other, n_exp), lax.rem(other, n_exp)),
            device_id_type=MESH,
        )
        return carry

    lax.fori_loop(1, n_dev, greet, 0)
    loads = [
        pltpu.make_async_copy(src, dst, in_sem.at[at])
        for at, (src, dst) in enumerate(
            ((gate_hbm, gate_ref), (idx_hbm, idx_ref), (acts_hbm, acts_ref), (w_hbm, w_buf))
        )
    ]
    for load in loads:
        load.start()
    for copy in own_grads:
        copy.wait()
    pl.semaphore_wait(barrier, n_dev - 1)

    def grad_copy(p, slot, sem, yy, ee):
        block = grads.at[p, slot]
        return pltpu.make_async_remote_copy(
            src_ref=block, dst_ref=block, send_sem=sem, recv_sem=g_recv.at[p, slot],
            device_id=dev(yy, ee), device_id_type=MESH,
        )

    def arrived(p, slot):
        grad_copy(p, slot, c_send.at[p, 0], y, expert_of(x, z, 1 - c)).wait_recv()

    sent = []

    def send(copy, when=None):
        if when is None:
            copy.start()
        else:
            pl.when(when)(copy.start)
        sent.append((when, copy))

    def pass_on(p, yy, xx, zz, to_x, to_y, when=None):
        slot = slot_of(yy, xx, zz, c)
        in_plane = xx * ZS + zz
        if to_x:
            at = zz if yy is y else ZS
            send(grad_copy(p, slot, x_send.at[p, at], y, expert_of(1 - x, z, c)), when)
        if to_y:
            send(grad_copy(p, slot, y_send.at[p, in_plane], 1 - y, me), when)
        at = yy * XS * ZS + in_plane
        send(grad_copy(p, slot, c_send.at[p, at], y, expert_of(x, z, 1 - c)), when)

    def along_z(p, zz, way, when):
        slot = slot_of(y, x, zz, c)
        sem = z_send.at[p, (way + 1) // 2, zz]
        send(grad_copy(p, slot, sem, y, expert_of(x, z + way, c)), when)

    for p in range(PARTS):
        for way in (1, -1):
            along_z(p, z, way, (z + way >= 0) & (z + way < ZS))
        pass_on(p, y, x, z, True, True)

    for load in loads[:3]:
        load.wait()
    gate = gate_ref[...]
    gate_half = gate.astype(jnp.bfloat16).astype(jnp.float32)
    idx = idx_ref[...].astype(jnp.float32)
    lane = lax.broadcasted_iota(jnp.int32, (tok, routed), 1)
    line = lax.broadcasted_iota(jnp.int32, (tok, routed), 0)
    widen = (lax.div(lane, top) == line).astype(jnp.float32)
    own_row = lax.broadcasted_iota(jnp.int32, (top, routed), 0) == lax.rem(
        lax.broadcasted_iota(jnp.int32, (top, routed), 1), top
    )
    gate_row = jnp.sum(
        jnp.where(own_row, jnp.dot(gate_half, widen, preferred_element_type=jnp.float32), 0.0),
        axis=0, keepdims=True,
    )
    idx_row = jnp.sum(
        jnp.where(own_row, jnp.dot(idx, widen, preferred_element_type=jnp.float32), 0.0),
        axis=0, keepdims=True,
    )
    rows = n_exp * tok
    row = lax.broadcasted_iota(jnp.int32, (rows, routed), 0)
    col = lax.broadcasted_iota(jnp.int32, (rows, routed), 1)
    row_exp = lax.div(row, tok).astype(jnp.float32)
    place = jnp.where(
        (idx_row == row_exp) & (lax.div(col, top) == lax.rem(row, tok)), gate_row, 0.0
    ).astype(jnp.bfloat16)
    weighted = jnp.dot(place, acts_ref[...], preferred_element_type=jnp.float32)
    weighted = weighted.astype(jnp.bfloat16).reshape(n_exp, tok, width)
    acts_send[0] = weighted[:, :, :half]
    acts_send[1] = weighted[:, :, half:]

    tall_row = lax.broadcasted_iota(jnp.int32, (routed, tok), 0)
    tall_col = lax.broadcasted_iota(jnp.int32, (routed, tok), 1)
    spread = (lax.div(tall_row, top) == tall_col).astype(jnp.float32)
    own_k = (
        lax.broadcasted_iota(jnp.int32, (routed, top), 1)
        == lax.rem(lax.broadcasted_iota(jnp.int32, (routed, top), 0), top)
    ).astype(jnp.float32)

    def column(of):
        wide = lax.dot_general(
            spread, of, (((1,), (1,)), ((), ())), preferred_element_type=jnp.float32
        )
        return jnp.sum(wide * own_k, axis=1, keepdims=True)

    gate_col = column(gate_half)
    idx_col = column(idx)
    row = lax.broadcasted_iota(jnp.int32, (routed, rows), 0)
    col = lax.broadcasted_iota(jnp.int32, (routed, rows), 1)
    pick = (
        (idx_col == lax.div(col, tok).astype(jnp.float32))
        & (lax.div(row, top) == lax.rem(col, tok))
    ).astype(jnp.float32).astype(jnp.bfloat16)

    def receive(p, yy, xx, dist, to_z, to_x, to_y):
        for way in (1, -1) if dist else (1,):
            zz = z - way * dist
            there = (zz >= 0) & (zz < ZS) if dist else None
            slot = slot_of(yy, xx, zz, c)
            if dist:
                pl.when(there)(functools.partial(arrived, p, slot))
            else:
                arrived(p, slot)
            if to_z:
                along_z(p, zz, way, there & (z + way >= 0) & (z + way < ZS))
            pass_on(p, yy, xx, zz, to_x, to_y, there)

    def from_z(p, dist):
        receive(p, y, x, dist, True, True, True)

    def from_x(p, dist):
        receive(p, y, 1 - x, dist, False, False, dist != 2)

    def from_group(p, xx, dist):
        receive(p, 1 - y, xx, dist, False, xx is x and dist == 2, False)

    def acts_copy(r):
        other = lax.rem(lid + r, n_dev)
        yy, ee = lax.div(other, n_exp), lax.rem(other, n_exp)
        return pltpu.make_async_remote_copy(
            src_ref=acts_send.at[yy, ee], dst_ref=acts_in.at[own],
            send_sem=h_send.at[r], recv_sem=h_recv.at[own],
            device_id=dev(yy, ee), device_id_type=MESH,
        )

    def acts_start(r, carry):
        acts_copy(r).start()
        return carry

    own_acts = pltpu.make_async_copy(acts_send.at[y, me], acts_in.at[own], own_sem.at[1])

    def back_copy(slot, zz, xx, cc):
        return pltpu.make_async_remote_copy(
            src_ref=hid.at[slot], dst_ref=back.at[me],
            send_sem=b_send.at[slot], recv_sem=b_recv.at[me],
            device_id=dev(y, expert_of(xx, zz, cc)), device_id_type=MESH,
        )

    per_x = ZS * CS
    tile = model // 4

    def hidden(p):
        part = lax.dot_general(
            grads[p, pl.ds(y * n_exp, n_exp)].reshape(n_exp * tok, part_cols),
            w_buf[:, pl.ds(p * part_cols, part_cols)],
            (((1,), (1,)), ((), ())), preferred_element_type=jnp.float32,
        )
        if p:
            part = part + hid_sum[...]
        if p < PARTS - 1:
            hid_sum[...] = part
        else:
            hid[...] = part.astype(jnp.bfloat16).reshape(n_exp, tok, width)

    def mates(p, group):
        for xx in (x, 1 - x):
            for zz in range(ZS):
                arrived(p, slot_of(group, xx, zz, 1 - c))

    parts = range(PARTS)
    for p in parts:
        from_z(p, 1)
    for p in parts:
        from_x(p, 0)
    for p in parts:
        from_z(p, 2)
    for p in parts:
        from_x(p, 1)
    for p in parts:
        from_z(p, 3)
    lax.fori_loop(1, n_dev, acts_start, 0)
    own_acts.start()
    for p in parts:
        from_x(p, 2)
    for dist in range(2):
        for p in parts:
            from_group(p, x, dist)
    loads[3].wait()
    for p in parts:
        from_x(p, 3)
        mates(p, y)
        hidden(p)
    own_back = pltpu.make_async_copy(hid.at[own - y * n_exp], back.at[me], own_sem.at[0])
    own_back.start()

    def each_back():
        for xx in (1 - x, x):
            for r in range(per_x):
                at = lax.rem(z * CS + c + r, per_x)
                if xx is not x or r:
                    yield back_copy(xx * per_x + at, lax.div(at, CS), xx, lax.rem(at, CS))

    for copy in each_back():
        copy.start()

    def acts_wait(r, group):
        ee = lax.rem(me + r, n_exp)
        slot = slot_of(
            group, lax.rem(lax.div(ee, CS), XS), lax.div(ee, XS * CS), lax.rem(ee, CS)
        )
        pltpu.make_async_remote_copy(
            src_ref=acts_send.at[0, 0], dst_ref=acts_in.at[slot],
            send_sem=h_send.at[0], recv_sem=h_recv.at[slot],
            device_id=dev(1 - y, me), device_id_type=MESH,
        ).wait_recv()
        return group

    def turn(group, at):
        rows_in = acts_in[pl.ds(group * n_exp, n_exp)].reshape(n_exp * tok, half)
        acts_t[at] = rows_in.T

    def down_part(group, at, n):
        p = lax.div(n * tile, part_cols)
        cols = pl.ds(pl.multiple_of(lax.rem(n * tile, part_cols), tile), tile)
        return jnp.dot(
            acts_t[at], grads[p, pl.ds(group * n_exp, n_exp), :, cols].reshape(n_exp * tok, tile),
            preferred_element_type=jnp.float32,
        )

    for dist in range(2, ZS):
        for p in parts:
            from_group(p, x, dist)

    lax.fori_loop(1, n_exp, acts_wait, y)
    own_acts.wait()
    turn(y, 0)

    @pl.loop(0, model // tile)
    def _(n):
        cols = pl.ds(pl.multiple_of(n * tile, tile), tile)
        total[:, cols] = down_part(y, 0, n)

    for dist in range(ZS):
        for p in parts:
            from_group(p, 1 - x, dist)

    lax.fori_loop(0, n_exp, acts_wait, 1 - y)
    turn(1 - y, 1)
    for p in parts:
        mates(p, 1 - y)

    @pl.loop(0, model // tile)
    def _(n):
        cols = pl.ds(pl.multiple_of(n * tile, tile), tile)
        down_out[:, cols] = (total[:, cols] + down_part(1 - y, 1, n)).astype(jnp.bfloat16)

    def back_wait(r, carry):
        ee = lax.rem(me + r, n_exp)
        pltpu.make_async_remote_copy(
            src_ref=hid.at[0], dst_ref=back.at[ee],
            send_sem=b_send.at[0], recv_sem=b_recv.at[ee],
            device_id=dev(1 - y, me), device_id_type=MESH,
        ).wait_recv()
        return carry

    lax.fori_loop(1, n_exp, back_wait, 0)
    own_back.wait()
    picked = jnp.dot(pick, back[...].reshape(rows, width), preferred_element_type=jnp.float32)
    act_out[...] = (gate_col * picked).astype(jnp.bfloat16)
    score = jnp.sum(picked * acts_ref[...].astype(jnp.float32), axis=1, keepdims=True)
    score = score.astype(jnp.bfloat16).astype(jnp.float32)
    score = jnp.dot(own_row.astype(jnp.float32), score * spread, preferred_element_type=jnp.float32)
    logit_out[...] = gate * (score - jnp.sum(gate * score, axis=0, keepdims=True))

    for when, copy in sent:
        if when is None:
            copy.wait_send()
        else:
            pl.when(when)(copy.wait_send)

    def acts_sent(r, carry):
        acts_copy(r).wait_send()
        return carry

    lax.fori_loop(1, n_dev, acts_sent, 0)
    for copy in each_back():
        copy.wait_send()


def store_kernel(*refs):
    results, outs, sems = refs[:3], refs[3:6], refs[6]
    copies = []
    for src, dst in zip(results, outs):
        rows = src.shape[0]
        step = rows // STRIPS if rows % (16 * STRIPS) == 0 else rows
        for at in range(0, rows, step):
            strip = pl.ds(at, step)
            copies.append(
                pltpu.make_async_copy(src.at[strip], dst.at[strip], sems.at[len(copies)])
            )
    for copy in copies[::-1]:
        copy.start()
    for copy in copies:
        copy.wait()


def gathered_shards(out_grad, hidden_acts, gate_weights, expert_idx, down_weight):
    tok, top = expert_idx.shape
    model = out_grad.shape[1]
    width = hidden_acts.shape[2]
    half = width // 2
    n_exp = ZS * XS * CS
    n_dev = 2 * n_exp
    dma = pltpu.SemaphoreType.DMA
    vmem = pl.BlockSpec(memory_space=pltpu.VMEM)
    hbm = pl.BlockSpec(memory_space=pltpu.HBM)
    act, logit, down = pl.pallas_call(
        gather_kernel,
        out_shape=(
            jax.ShapeDtypeStruct((tok * top, width), jnp.bfloat16),
            jax.ShapeDtypeStruct((top, tok), jnp.float32),
            jax.ShapeDtypeStruct((half, model), jnp.bfloat16),
        ),
        in_specs=[hbm] * 5,
        out_specs=(vmem, vmem, vmem),
        scratch_shapes=[
            pltpu.VMEM((top, tok), jnp.float32),
            pltpu.VMEM((top, tok), jnp.int32),
            pltpu.VMEM((tok * top, width), jnp.bfloat16),
            pltpu.VMEM((PARTS, n_dev, tok, model // PARTS), jnp.bfloat16),
            pltpu.VMEM((width, model), jnp.bfloat16),
            pltpu.VMEM((2, n_exp, tok, half), jnp.bfloat16),
            pltpu.VMEM((n_dev, tok, half), jnp.bfloat16),
            pltpu.VMEM((2, half, n_exp * tok), jnp.bfloat16),
            pltpu.VMEM((n_exp, tok, width), jnp.bfloat16),
            pltpu.VMEM((n_exp * tok, width), jnp.float32),
            pltpu.VMEM((n_exp, tok, width), jnp.bfloat16),
            pltpu.VMEM((half, model), jnp.float32),
            dma((4,)),
            dma((2 + PARTS,)),
            dma((PARTS, n_dev)),
            dma((PARTS, 2, ZS)),
            dma((PARTS, ZS + 1)),
            dma((PARTS, XS * ZS)),
            dma((PARTS, 2 * XS * ZS)),
            dma((n_dev,)),
            dma((n_dev,)),
            dma((n_exp,)),
            dma((n_exp,)),
        ],
        compiler_params=pltpu.CompilerParams(
            collective_id=0, has_side_effects=True, vmem_limit_bytes=36 * 1024 * 1024
        ),
        cost_estimate=pl.CostEstimate(
            flops=6 * n_exp * tok * model * width, bytes_accessed=3 * width * model * 2,
            transcendentals=0,
        ),
    )(
        *(
            pltpu.with_memory_space_constraint(array, pltpu.HBM)
            for array in (
                gate_weights.T, expert_idx.T, hidden_acts.reshape(tok * top, width), out_grad,
                down_weight.reshape(width, model),
            )
        )
    )
    results = (act, logit, down)
    act, logit, down = pl.pallas_call(
        store_kernel,
        out_shape=tuple(jax.ShapeDtypeStruct(of.shape, of.dtype) for of in results),
        in_specs=[vmem] * 3,
        out_specs=(hbm,) * 3,
        scratch_shapes=[dma((3 * STRIPS,))],
        compiler_params=pltpu.CompilerParams(vmem_limit_bytes=16 * 1024 * 1024),
    )(*results)
    return act.reshape(tok, top, width), logit.T, down[None]


def solution(mesh):
    gathered = mesh.shape["dp"] == 2 and mesh.shape["expert"] == ZS * XS * CS
    return jax.shard_map(
        gathered_shards if gathered else routed_shards,
        mesh=mesh,
        in_specs=(
            P(("dp", "expert"), None),
            P(("dp", "expert"), None, None),
            P(("dp", "expert"), None),
            P(("dp", "expert"), None),
            P("expert", None, None),
        ),
        out_specs=(
            P(("dp", "expert"), None, None),
            P(("dp", "expert"), None),
            P("expert", "dp", None),
        ),
        check_vma=False,
    )
```
